32 devices in a mesh: modes: 8 (over y, x, core), tiles: 4 (over z).
Axes of the slice: x: 2, y: 2, z: 4, core: 2. Of those that a mesh axis runs over, the one named last changes fastest.
Arguments:
- solution_modes: float32 [512, 16, 8, 128], P('modes', 'tiles'), may hold values from -6 to 6
- coefficient_modes: float32 [128, 16, 8, 128], P('modes', 'tiles'), may hold values from 0.5 to 4
- coupling: float32 [16, 32, 32, 32], P('modes'), may hold values from -0.03125 to 0.03125
- source_block: int32 [16, 32], P('modes'), may hold values from 0 to 15
- expansion_index: int32 [16, 32], P('modes'), may hold values from 0 to 127
Outputs:
- applied: float32 [512, 16, 8, 128], P('modes', 'tiles')
The draws below stay inside these ranges and needn't reach their ends.
All inputs are finite; a program needn't handle non-finite values.
Results may differ from the reference program's by a relative error of at most 0.0003.
Values sent between devices are 32-bit elements; how exact they have to be, the bound alone decides.
No kernel may reach another device: no remote copies, remote signals or barrier semaphores. Data moves between devices by JAX's collectives and lax.ppermute only.
A program may use at most 128 MiB of HBM per device.

```python
import math
import jax
import jax.numpy as jnp
from jax import lax

P_SIZE = 512
K = 128
MB = 32
S = 32
NY = 8
NZ = 128
NBLK = 16
NX = 16


def touch_ends(array, stream_key, least, high):
    longest = array.shape.index(max(array.shape))
    spots = []
    for shift in (0, 1):
        where = [jax.random.randint(jax.random.fold_in(stream_key, axis), (), 0, length) for axis, length in enumerate(array.shape)]
        where[longest] = (where[longest] + shift) % array.shape[longest]
        spots.append(tuple(where))
    return array.at[spots[0]].set(least).at[spots[1]].set(high)


def shard_levels(rng, dims, pieces, low, largest):
    factor_of, own = 1.0, jax.random.fold_in(rng, 6)
    for axis_at, blocks in pieces:
        heights = jnp.exp(jax.random.uniform(jax.random.fold_in(own, axis_at), (blocks,), jnp.float32, low / len(pieces), largest / len(pieces)))
        factor_of = factor_of * jnp.repeat(heights, dims[axis_at] // blocks).reshape([-1 if axis == axis_at else 1 for axis in range(len(dims))])
    return factor_of


def bell_draw(stream_key, dims, spread, limit, split=(), kind=jnp.bfloat16):
    level = shard_levels(stream_key, dims, split, -0.22, 0.18) if split else 1.0
    values = jax.random.normal(stream_key, dims, jnp.float32) * spread * level
    return jnp.minimum(jnp.maximum(values, -limit), limit).astype(kind)


def setup_inputs(seed: int = 0) -> dict:
    streams_of = jax.random.split(jax.random.key(seed), 6)
    return {
        "solution_modes": bell_draw(streams_of[0], (P_SIZE, NX, NY, NZ), 1.0, 6.0, ((0, 8), (1, 4)), jnp.float32),
        "coefficient_modes": jnp.clip(jnp.exp(math.log(4.0) - 2.0794415 * jax.random.uniform(streams_of[1], (K, NX, NY, NZ), jnp.float32) ** shard_levels(streams_of[1], (K, NX, NY, NZ), ((0, 8), (1, 4)), -0.2, 0.2)), 0.5, 4.0),
        "coupling": bell_draw(streams_of[2], (NBLK, S, MB, MB), (40 * S * MB) ** -0.5, 0.03125, ((0, 8),), jnp.float32),
        "source_block": touch_ends(jax.random.randint(streams_of[3], (NBLK, S), 0, NBLK), jax.random.fold_in(streams_of[3], 1), 0, NBLK - 1).astype(jnp.int32),
        "expansion_index": touch_ends(jax.random.randint(streams_of[4], (NBLK, S), 0, K), jax.random.fold_in(streams_of[4], 1), 0, K - 1).astype(jnp.int32),
    }


def face_means(coefficient):
    along_first = 0.5 * (coefficient[:, :-1, 1:-1, 1:-1] + coefficient[:, 1:, 1:-1, 1:-1])
    along_second = 0.5 * (coefficient[:, 1:-1, :-1, 1:-1] + coefficient[:, 1:-1, 1:, 1:-1])
    along_third = 0.5 * (coefficient[:, 1:-1, 1:-1, :-1] + coefficient[:, 1:-1, 1:-1, 1:])
    return along_first, along_second, along_third


def divergence(blended, along_first, along_second, along_third):
    flux_first = along_first * (blended[:, :-1, 1:-1, 1:-1] - blended[:, 1:, 1:-1, 1:-1])
    flux_second = along_second * (blended[:, 1:-1, :-1, 1:-1] - blended[:, 1:-1, 1:, 1:-1])
    flux_third = along_third * (blended[:, 1:-1, 1:-1, :-1] - blended[:, 1:-1, 1:-1, 1:])
    result = flux_first[:, 1:] - flux_first[:, :-1]
    result = result + flux_second[:, :, 1:] - flux_second[:, :, :-1]
    return result + flux_third[:, :, :, 1:] - flux_third[:, :, :, :-1]


def block_output(padded_u, faces, coupling_rows, source_rows, expansion_rows, width):
    first_faces, second_faces, third_faces = faces
    shape = (width, padded_u.shape[1] - 2, padded_u.shape[2] - 2, padded_u.shape[3] - 2)

    def advance(running, slot_index):
        source = source_rows[slot_index].astype(jnp.int32)
        expansion = expansion_rows[slot_index].astype(jnp.int32)
        source_modes = lax.dynamic_slice_in_dim(padded_u, source * width, width, 0)
        block_matrix = coupling_rows[slot_index]
        blended = jnp.einsum("ij,jxyz->ixyz", block_matrix, source_modes, precision=lax.Precision.HIGHEST)
        term = divergence(blended,
                          lax.dynamic_index_in_dim(first_faces, expansion, 0, keepdims=False),
                          lax.dynamic_index_in_dim(second_faces, expansion, 0, keepdims=False),
                          lax.dynamic_index_in_dim(third_faces, expansion, 0, keepdims=False))
        return running + term, None

    start = jnp.zeros(shape, jnp.float32)
    total, _ = lax.scan(advance, start, jnp.arange(source_rows.shape[0], dtype=jnp.int32))
    return total


def reference(solution_modes, coefficient_modes, coupling, source_block, expansion_index):
    padding = ((0, 0), (1, 1), (1, 1), (1, 1))
    padded_u = jnp.pad(solution_modes, padding)
    padded_a = jnp.pad(coefficient_modes, padding)
    faces = face_means(padded_a)

    def one_block(block_index):
        return block_output(padded_u, faces, coupling[block_index], source_block[block_index],
                            expansion_index[block_index], MB)

    stacked = lax.map(one_block, jnp.arange(NBLK, dtype=jnp.int32))
    return stacked.reshape(solution_modes.shape)
```

```python
import functools

import jax
import jax.numpy as jnp
from jax import lax
from jax.experimental import pallas as pl
from jax.experimental.pallas import tpu as pltpu
from jax.sharding import PartitionSpec as P

VMEM_LIMIT = 56 * 1024 * 1024
CHUNK = 4


def lane_index(rows):
    return lax.broadcasted_iota(jnp.int32, (rows, 128), 1)


def swap_lanes(tiles, depth, lanes):
    tiles = list(tiles)
    size = len(tiles)
    step = 1
    while step < size:
        width = step * depth
        upper = (lanes & width) != 0
        for low in range(size):
            if low & step:
                continue
            high = low | step
            first, second = tiles[low], tiles[high]
            tiles[low] = jnp.where(upper, pltpu.roll(second, width, 1), first)
            tiles[high] = jnp.where(upper, second, pltpu.roll(first, 128 - width, 1))
        step *= 2
    return tiles


def turn(value, shift):
    shift = shift % 128
    return value if shift == 0 else pltpu.roll(value, shift, 1)


def pack_kernel(
    geometry, chip_ref, u_ref, a_ref, coupling_ref, index_ref, *rest
):
    layers, halves, ny, depth, chips = geometry
    sends, packs, stage = rest[:chips], rest[chips], rest[chips + 1]
    me = chip_ref[0]
    lanes = lane_index(8)
    place = lanes % depth
    row = 0
    for ref in (u_ref, a_ref):
        modes = ref.shape[0] // (layers * ny)

        def group(g, carry, ref=ref, row=row):
            target = pl.multiple_of(row + g * 8, 8)
            by_layer = []
            for x in range(layers):
                tiles = [
                    ref[pl.ds(g * 8 * layers * ny + x * ny + y, 8, stride=layers * ny), :]
                    for y in range(ny)
                ]
                tiles = swap_lanes(tiles, depth, lanes)
                by_layer.append(tiles)
                for d in range(ny):
                    stage[d // halves, x * halves + d % halves, pl.ds(target, 8), :] = tiles[d]
            for chip in range(chips):
                rim = jnp.zeros((8, 128), jnp.float32)
                left, right = chip * halves - 1, (chip + 1) * halves
                for x in range(layers):
                    if left >= 0:
                        rim = jnp.where(place == x, turn(by_layer[x][left], x + 1 - depth), rim)
                    if right < ny:
                        at = depth // 2 + x
                        rim = jnp.where(place == at, turn(by_layer[x][right], at), rim)
                stage[chip, layers * halves, pl.ds(target, 8), :] = rim
            return carry

        lax.fori_loop(0, modes // 8, group, 0)
        row += modes
    for e in range(chips):
        sends[e][...] = stage[e ^ me]
    blocks, slots, width, _ = coupling_ref.shape
    per = 128 // width
    groups = slots // per
    for block in range(blocks):

        def gather(g, carry, block=block):
            packs[block * groups + g] = jnp.concatenate(
                [coupling_ref[block, g * per + q] for q in range(per)], axis=1
            )
            return carry

        lax.fori_loop(0, groups, gather, 0)
    packs[blocks * groups] = index_ref[...]


def laplacian(tile, low, high, rim, geometry, rows):
    layers, halves, ny, depth, _ = geometry
    lanes = lane_index(rows)
    place = lanes % depth
    first_row, last_row = lanes < depth, lanes >= 128 - depth
    result = []
    for x in range(layers):
        result.append([])
        for h in range(halves):
            c = tile[x][h]
            before = tile[x - 1][h] if x else low[h]
            after = tile[x + 1][h] if x + 1 < layers else high[h]
            up = jnp.where(first_row, 0.0, turn(c, depth))
            down = jnp.where(last_row, 0.0, turn(c, -depth))
            edge = turn(tile[x][h - 1], 1 - depth) if h else turn(rim, -x)
            left = jnp.where(place == 0, edge, turn(c, 1))
            if h + 1 < halves:
                edge = turn(tile[x][h + 1], depth - 1)
            else:
                edge = turn(rim, depth - 1 - depth // 2 - x)
            right = jnp.where(place == depth - 1, edge, turn(c, -1))
            result[-1].append(((before + after) + (up + down)) + ((left + right) - 6.0 * c))
    return result


def halves_of(value):
    upper = value.astype(jnp.bfloat16)
    lower = (value - upper.astype(jnp.float32)).astype(jnp.bfloat16)
    return upper, lower


def apply_kernel(geometry, sizes, where_ref, source_ref, expansion_ref, *rest):
    layers, halves, ny, depth, chips = geometry
    blocks, width, slots, local_u, local_a = sizes
    tiles = layers * halves
    chunks = tiles // CHUNK
    span = CHUNK * 128
    rim_at = chunks * 2 * span
    take = lambda n: (rest[:n], rest[n:])
    bodies, rest = take(2 * chips)
    lows, rest = take(2)
    highs, rest = take(2)
    packs, rest = take(chips)
    out_ref, sources, fields, mix, product, cross = rest
    chip, core = where_ref[0], where_ref[1]

    def columns(t):
        base = (t // CHUNK) * 2 * span + (t % CHUNK) * 128
        return base, base + span

    def load(body, low, high, e, start, rows):
        part = pl.ds(start, rows)
        tile = [[body[x * halves + h, part, :] for h in range(halves)] for x in range(layers)]
        below = [low[e, h, part, :] for h in range(halves)]
        above = [high[e, h, part, :] for h in range(halves)]
        return tile, below, above, body[tiles, part, :]

    for side in range(2):
        for e in range(chips):
            body, low, high = bodies[side * chips + e], lows[side], highs[side]
            device = (chip ^ e) * 2 + (core ^ side)

            def prepare_u(g, carry, body=body, low=low, high=high, e=e, device=device):
                start = pl.multiple_of(g * 16, 16)
                tile, below, above, rim = load(body, low, high, e, start, 16)
                lap = laplacian(tile, below, above, rim, geometry, 16)
                block = device * (local_u // width) + (g * 16) // width
                row = pl.multiple_of((g * 16) % width, 16)

                def put(value, at):
                    upper, lower = halves_of(value)
                    where = pl.ds(at, 128)
                    sources[block, pl.ds(row, 16), where] = upper
                    sources[block, pl.ds(width + row, 16), where] = lower
                    sources[block, pl.ds(2 * width + row, 16), where] = upper

                for t in range(tiles):
                    x, h = t // halves, t % halves
                    put(tile[x][h], columns(t)[0])
                    put(lap[x][h], columns(t)[1])
                for h in range(halves):
                    put(below[h], rim_at + h * 128)
                    put(above[h], rim_at + (halves + h) * 128)
                put(rim, rim_at + 2 * halves * 128)
                return carry

            lax.fori_loop(0, local_u // 16, prepare_u, 0)
            tile, below, above, rim = load(body, low, high, e, local_u, local_a)
            lap = laplacian(tile, below, above, rim, geometry, local_a)
            rows = pl.ds(pl.multiple_of(device * local_a, local_a), local_a)
            for t in range(tiles):
                x, h = t // halves, t % halves
                fields[rows, pl.ds(columns(t)[0], 128)] = tile[x][h]
                fields[rows, pl.ds(columns(t)[1], 128)] = lap[x][h]
            for h in range(halves):
                fields[rows, pl.ds(rim_at + h * 128, 128)] = below[h]
                fields[rows, pl.ds(rim_at + (halves + h) * 128, 128)] = above[h]
            fields[rows, pl.ds(rim_at + 2 * halves * 128, 128)] = rim

    per = 128 // width
    groups = slots // per
    for e in range(chips):

        def spread(n, carry, e=e):
            value = packs[e][n]
            upper = value.astype(jnp.bfloat16).astype(jnp.float32)
            lower = value - upper
            for q in range(per):
                lanes = slice(q * width, (q + 1) * width)
                part = jnp.concatenate([upper[:, lanes], upper[:, lanes], lower[:, lanes]], axis=1)
                mix[e * blocks * slots + n * per + q] = part.astype(jnp.bfloat16)
            return carry

        lax.fori_loop(0, blocks * groups, spread, 0)

    rims = (2 * halves + 1) * 128

    def one_block(n, carry):
        for chunk in range(chunks):
            base = chunk * 2 * span

            def step(s, totals, base=base):
                total, rest_total = totals
                at = n * slots + s
                j, k = source_ref[at], expansion_ref[at]
                mixed = jnp.dot(
                    mix[at],
                    sources[j, :, base : base + 2 * span],
                    preferred_element_type=jnp.float32,
                )
                field = fields[pl.ds(k, 1), base : base + span]
                bent = fields[pl.ds(k, 1), base + span : base + 2 * span]
                value, curve = mixed[:, :span], mixed[:, span:]
                return total + field * value, rest_total + (bent * value - field * curve)

            zero = jnp.zeros((width, span), jnp.float32)
            total, rest_total = lax.fori_loop(0, slots, step, (zero, zero), unroll=4)
            for i in range(CHUNK):
                product[chunk * CHUNK + i] = total[:, i * 128 : (i + 1) * 128]
                cross[chunk * CHUNK + i] = rest_total[:, i * 128 : (i + 1) * 128]

        def rim_step(s, total):
            at = n * slots + s
            j, k = source_ref[at], expansion_ref[at]
            mixed = jnp.dot(
                mix[at],
                sources[j, :, rim_at : rim_at + rims],
                preferred_element_type=jnp.float32,
            )
            return total + fields[pl.ds(k, 1), rim_at : rim_at + rims] * mixed

        total = lax.fori_loop(0, slots, rim_step, jnp.zeros((width, rims), jnp.float32), unroll=4)
        for i in range(2 * halves + 1):
            product[tiles + i] = total[:, i * 128 : (i + 1) * 128]

        for r in range(0, width, 8):
            part = slice(r, r + 8)
            tile = [[product[x * halves + h, part, :] for h in range(halves)] for x in range(layers)]
            low = [product[tiles + h, part, :] for h in range(halves)]
            high = [product[tiles + halves + h, part, :] for h in range(halves)]
            rim = product[tiles + 2 * halves, part, :]
            lap = laplacian(tile, low, high, rim, geometry, 8)
            for t in range(tiles):
                row = pl.multiple_of((n % blocks) * width + r, 8)
                out_ref[n // blocks, t, pl.ds(row, 8), :] = 0.5 * (
                    cross[t, part, :] - lap[t // halves][t % halves]
                )
        return carry

    lax.fori_loop(0, chips * blocks, one_block, 0)


def unpack_kernel(geometry, chip_ref, *rest):
    layers, halves, ny, depth, chips = geometry
    parts, out_ref, stage = rest[:chips], rest[chips], rest[chips + 1]
    me = chip_ref[0]
    for e in range(chips):
        stage[e ^ me] = parts[e][...]
    lanes = lane_index(8)
    modes = out_ref.shape[0] // (layers * ny)

    def group(g, carry):
        source = pl.multiple_of(g * 8, 8)
        for x in range(layers):
            tiles = [
                stage[d // halves, x * halves + d % halves, pl.ds(source, 8), :] for d in range(ny)
            ]
            tiles = swap_lanes(tiles, depth, lanes)
            for y in range(ny):
                out_ref[pl.ds(g * 8 * layers * ny + x * ny + y, 8, stride=layers * ny), :] = tiles[y]
        return carry

    lax.fori_loop(0, modes // 8, group, 0)


def vmem(count):
    return [pl.BlockSpec(memory_space=pltpu.VMEM)] * count


def smem(count):
    return [pl.BlockSpec(memory_space=pltpu.SMEM)] * count


def on_device(solution_modes, coefficient_modes, coupling, source_block, expansion_index):
    local_u, layers, ny, nz = solution_modes.shape
    local_a = coefficient_modes.shape[0]
    blocks, slots, width = coupling.shape[:3]
    count = lax.axis_size("modes")
    chips = count // 2
    depth = 128 // ny
    halves = (nz // depth) // chips
    geometry = (layers, halves, ny, depth, chips)
    tiles = layers * halves
    modes = local_u + local_a
    me = lax.axis_index("modes")
    chip, core = me // 2, me % 2
    f32 = jnp.float32
    params = pltpu.CompilerParams(vmem_limit_bytes=VMEM_LIMIT)

    flat = jnp.stack([source_block, expansion_index]).astype(f32).reshape(-1)
    indices = jnp.zeros((width * 128,), f32).at[: flat.size].set(flat).reshape(width, 128)
    per = 128 // width
    groups = slots // per
    packed = pl.pallas_call(
        functools.partial(pack_kernel, geometry),
        out_shape=[jax.ShapeDtypeStruct((tiles + 1, modes, 128), f32)] * chips
        + [jax.ShapeDtypeStruct((blocks * groups + 1, width, 128), f32)],
        in_specs=smem(1) + vmem(4),
        out_specs=vmem(chips + 1),
        scratch_shapes=[pltpu.VMEM((chips, tiles + 1, modes, 128), f32)],
        compiler_params=params,
        name="pack",
    )(
        chip[None],
        solution_modes.reshape(-1, nz),
        coefficient_modes.reshape(-1, nz),
        coupling,
        indices,
    )
    sends, pack = packed[:chips], packed[chips]

    def trade(value, e):
        return lax.ppermute(value, "modes", [(i, i ^ (2 * e)) for i in range(count)])

    def sibling(value):
        return lax.ppermute(value, "modes", [(i, i ^ 1) for i in range(count)])

    packs = [pack] + [trade(pack, e) for e in range(1, chips)]
    bodies = [sends[0]] + [trade(sends[e], e) for e in range(1, chips)]
    n_tiles = lax.axis_size("tiles")
    up = [(i, i + 1) for i in range(n_tiles - 1)]
    down = [(i + 1, i) for i in range(n_tiles - 1)]
    bottom = jnp.stack([body[:halves] for body in bodies])
    top = jnp.stack([body[tiles - halves : tiles] for body in bodies])
    low, high = lax.ppermute(top, "tiles", up), lax.ppermute(bottom, "tiles", down)
    bodies = bodies + [sibling(body) for body in bodies]
    low_other, high_other = sibling(low), sibling(high)

    numbers = jnp.stack([p[blocks * groups] for p in packs]).reshape(chips, -1)
    numbers = numbers[:, : 2 * blocks * slots].astype(jnp.int32).reshape(chips, 2, blocks * slots)
    sources = numbers[:, 0].reshape(-1)
    expansions = numbers[:, 1].reshape(-1)

    ncol = 2 * tiles * 128 + (2 * halves + 1) * 128
    n_blocks = chips * 2 * (local_u // width)
    result = pl.pallas_call(
        functools.partial(
            apply_kernel, geometry, (blocks, width, slots, local_u, local_a)
        ),
        out_shape=jax.ShapeDtypeStruct((chips, tiles, local_u, 128), f32),
        in_specs=smem(3) + vmem(2 * chips + 4 + chips),
        out_specs=pl.BlockSpec(memory_space=pltpu.VMEM),
        scratch_shapes=[
            pltpu.VMEM((n_blocks, 3 * width, ncol), jnp.bfloat16),
            pltpu.VMEM((chips * 2 * local_a, ncol), f32),
            pltpu.VMEM((chips * blocks * slots, width, 3 * width), jnp.bfloat16),
            pltpu.VMEM((tiles + 2 * halves + 1, width, 128), f32),
            pltpu.VMEM((tiles, width, 128), f32),
        ],
        compiler_params=params,
        name="apply",
    )(
        jnp.stack([chip, core]),
        sources,
        expansions,
        *bodies,
        low,
        low_other,
        high,
        high_other,
        *packs,
    )
    parts = [result[0]] + [trade(result[e], e) for e in range(1, chips)]
    out = pl.pallas_call(
        functools.partial(unpack_kernel, geometry),
        out_shape=jax.ShapeDtypeStruct((local_u * layers * ny, nz), f32),
        in_specs=smem(1) + vmem(chips),
        out_specs=pl.BlockSpec(memory_space=pltpu.VMEM),
        scratch_shapes=[pltpu.VMEM((chips, tiles, local_u, 128), f32)],
        compiler_params=params,
        name="unpack",
    )(chip[None], *parts)
    return out.reshape(solution_modes.shape)


def solution(mesh):
    placed = (
        P("modes", "tiles", None, None),
        P("modes", "tiles", None, None),
        P("modes", None, None, None),
        P("modes", None),
        P("modes", None),
    )
    return jax.shard_map(
        on_device,
        mesh=mesh,
        in_specs=placed,
        out_specs=P("modes", "tiles", None, None),
        check_vma=False,
    )
```

```python
import functools

import jax
import jax.numpy as jnp
from jax import lax
from jax.experimental import pallas as pl
from jax.experimental.pallas import tpu as pltpu
from jax.sharding import PartitionSpec as P

PACK_LIMIT = 16
PREPARE_LIMIT = 24
APPLY_LIMIT = 24
CHUNK = 4


def lane_index(rows):
    return lax.broadcasted_iota(jnp.int32, (rows, 128), 1)


def swap_lanes(tiles, depth, lanes):
    tiles = list(tiles)
    size = len(tiles)
    step = 1
    while step < size:
        width = step * depth
        upper = (lanes & width) != 0
        for low in range(size):
            if low & step:
                continue
            high = low | step
            first, second = tiles[low], tiles[high]
            tiles[low] = jnp.where(upper, pltpu.roll(second, width, 1), first)
            tiles[high] = jnp.where(upper, second, pltpu.roll(first, 128 - width, 1))
        step *= 2
    return tiles


def turn(value, shift):
    shift = shift % 128
    return value if shift == 0 else pltpu.roll(value, shift, 1)


def pack_fields(geometry, u_ref, a_ref, *rest):
    layers, halves, ny, depth, chips = geometry
    sends, stage = rest[:chips], rest[chips]
    me = lax.axis_index("modes") // 2
    lanes = lane_index(8)
    place = lanes % depth
    row = 0
    for ref in (u_ref, a_ref):
        modes = ref.shape[0] // (layers * ny)

        def group(g, carry, ref=ref, row=row):
            target = pl.multiple_of(row + g * 8, 8)
            by_layer = []
            for x in range(layers):
                tiles = [
                    ref[pl.ds(g * 8 * layers * ny + x * ny + y, 8, stride=layers * ny), :]
                    for y in range(ny)
                ]
                tiles = swap_lanes(tiles, depth, lanes)
                by_layer.append(tiles)
                for d in range(ny):
                    stage[d // halves, x * halves + d % halves, pl.ds(target, 8), :] = tiles[d]
            for chip in range(chips):
                rim = jnp.zeros((8, 128), jnp.float32)
                left, right = chip * halves - 1, (chip + 1) * halves
                for x in range(layers):
                    if left >= 0:
                        rim = jnp.where(place == x, turn(by_layer[x][left], x + 1 - depth), rim)
                    if right < ny:
                        at = depth // 2 + x
                        rim = jnp.where(place == at, turn(by_layer[x][right], at), rim)
                stage[chip, layers * halves, pl.ds(target, 8), :] = rim
            return carry

        lax.fori_loop(0, modes // 8, group, 0)
        row += modes
    for e in range(chips):
        sends[e][...] = stage[e ^ me]


def pack_coupling(coupling_ref, source_ref, expansion_ref, out_ref):
    blocks, slots, width, _ = coupling_ref.shape
    per = 128 // width
    groups = slots // per
    for block in range(blocks):
        for g in range(groups):
            rows = slice((block * groups + g) * width, (block * groups + g + 1) * width)
            out_ref[rows, :] = jnp.concatenate(
                [coupling_ref[block, g * per + q] for q in range(per)], axis=1
            )
    last = blocks * groups * width
    out_ref[last : last + 8, :] = jnp.zeros((8, 128), jnp.float32)
    out_ref[last : last + blocks, 0:slots] = source_ref[...].astype(jnp.float32)
    out_ref[last + blocks : last + 2 * blocks, 0:slots] = expansion_ref[...].astype(jnp.float32)


def laplacian(tile, low, high, rim, geometry, rows):
    layers, halves, ny, depth, _ = geometry
    lanes = lane_index(rows)
    place = lanes % depth
    first_row, last_row = lanes < depth, lanes >= 128 - depth
    result = []
    for x in range(layers):
        result.append([])
        for h in range(halves):
            c = tile[x][h]
            before = tile[x - 1][h] if x else low[h]
            after = tile[x + 1][h] if x + 1 < layers else high[h]
            up = jnp.where(first_row, 0.0, turn(c, depth))
            down = jnp.where(last_row, 0.0, turn(c, -depth))
            edge = turn(tile[x][h - 1], 1 - depth) if h else turn(rim, -x)
            left = jnp.where(place == 0, edge, turn(c, 1))
            if h + 1 < halves:
                edge = turn(tile[x][h + 1], depth - 1)
            else:
                edge = turn(rim, depth - 1 - depth // 2 - x)
            right = jnp.where(place == depth - 1, edge, turn(c, -1))
            result[-1].append(((before + after) + (up + down)) + ((left + right) - 6.0 * c))
    return result


def halves_of(value):
    upper = value.astype(jnp.bfloat16)
    lower = (value - upper.astype(jnp.float32)).astype(jnp.bfloat16)
    return upper, lower


def columns(tile, tiles):
    base = (tile // CHUNK) * 2 * CHUNK * 128 + (tile % CHUNK) * 128
    return base, base + CHUNK * 128


def prepare_kernel(geometry, width, local_u, local_a, e, *rest):
    layers, halves, ny, depth, chips = geometry
    body_refs, low_refs, high_refs = rest[0:2], rest[2:4], rest[4:6]
    sources, fields = rest[-2:]
    tiles = layers * halves
    rim_at = 2 * tiles * 128
    me = lax.axis_index("modes")

    for side in range(2):
        body, low, high = body_refs[side], low_refs[side], high_refs[side]
        device = me ^ (2 * e) ^ side

        def load(start, rows, body=body, low=low, high=high):
            part = pl.ds(start, rows)
            tile = [[body[x * halves + h, part, :] for h in range(halves)] for x in range(layers)]
            below = [low[h, part, :] for h in range(halves)]
            above = [high[h, part, :] for h in range(halves)]
            return tile, below, above, body[tiles, part, :]

        def prepare_u(g, carry, load=load, device=device):
            start = pl.multiple_of(g * 16, 16)
            tile, below, above, rim = load(start, 16)
            lap = laplacian(tile, below, above, rim, geometry, 16)
            block = device * (local_u // width) + (g * 16) // width
            row = pl.multiple_of((g * 16) % width, 16)

            def put(value, at):
                upper, lower = halves_of(value)
                where = pl.ds(at, 128)
                sources[block, pl.ds(row, 16), where] = upper
                sources[block, pl.ds(width + row, 16), where] = lower
                sources[block, pl.ds(2 * width + row, 16), where] = upper

            for t in range(tiles):
                x, h = t // halves, t % halves
                put(tile[x][h], columns(t, tiles)[0])
                put(lap[x][h], columns(t, tiles)[1])
            for h in range(halves):
                put(below[h], rim_at + h * 128)
                put(above[h], rim_at + (halves + h) * 128)
            put(rim, rim_at + 2 * halves * 128)
            return carry

        lax.fori_loop(0, local_u // 16, prepare_u, 0)
        tile, below, above, rim = load(local_u, local_a)
        lap = laplacian(tile, below, above, rim, geometry, local_a)
        rows = pl.ds(pl.multiple_of(device * local_a, local_a), local_a)
        for t in range(tiles):
            x, h = t // halves, t % halves
            fields[rows, pl.ds(columns(t, tiles)[0], 128)] = tile[x][h]
            fields[rows, pl.ds(columns(t, tiles)[1], 128)] = lap[x][h]
        for h in range(halves):
            fields[rows, pl.ds(rim_at + h * 128, 128)] = below[h]
            fields[rows, pl.ds(rim_at + (halves + h) * 128, 128)] = above[h]
        fields[rows, pl.ds(rim_at + 2 * halves * 128, 128)] = rim


def apply_kernel(geometry, blocks, slots, width, pack, sources, fields, out_ref, mix, numbers, table, product, cross, sem):
    layers, halves, ny, depth, chips = geometry
    tiles = layers * halves
    chunks = tiles // CHUNK
    span = CHUNK * 128
    rim_at = 2 * tiles * 128
    rims = (2 * halves + 1) * 128
    per = 128 // width
    rows = blocks * slots // per * width

    numbers[...] = pack[rows : rows + 8, :].astype(jnp.int32)
    copy = pltpu.make_async_copy(numbers, table, sem)
    copy.start()
    value = pack[0:rows, :]
    upper, lower = halves_of(value)
    take = lax.broadcasted_iota(jnp.int32, (256, per * 128), 0)
    give = lax.broadcasted_iota(jnp.int32, (256, per * 128), 1)
    lane = give % 128
    wanted = (give // 128) * width + lane % width + jnp.where(lane >= 2 * width, 128, 0)
    chosen = jnp.where((take == wanted) & (lane < 3 * width), 1.0, 0.0).astype(jnp.bfloat16)
    mix[...] = jnp.dot(
        jnp.concatenate([upper, lower], axis=1), chosen, preferred_element_type=jnp.float32
    ).astype(jnp.bfloat16)
    copy.wait()

    def one_block(n, carry):
        def operands(s, first, count):
            j, k = table[n, s], table[blocks + n, s]
            group = pl.multiple_of((n * (slots // per) + s // per) * width, width)
            lanes = (s % per) * 128
            mixed = jnp.dot(
                mix[pl.ds(group, width), lanes : lanes + 3 * width],
                sources[j, :, first : first + count],
                preferred_element_type=jnp.float32,
            )
            return mixed, k

        for chunk in range(chunks):
            base = chunk * 2 * span
            total = jnp.zeros((width, span), jnp.float32)
            rest_total = jnp.zeros((width, span), jnp.float32)
            for s in range(slots):
                mixed, k = operands(s, base, 2 * span)
                field = fields[pl.ds(k, 1), base : base + span]
                bent = fields[pl.ds(k, 1), base + span : base + 2 * span]
                value, curve = mixed[:, :span], mixed[:, span:]
                total = total + field * value
                rest_total = rest_total + (bent * value - field * curve)
            for i in range(CHUNK):
                product[chunk * CHUNK + i] = total[:, i * 128 : (i + 1) * 128]
                cross[chunk * CHUNK + i] = rest_total[:, i * 128 : (i + 1) * 128]

        total = jnp.zeros((width, rims), jnp.float32)
        for s in range(slots):
            mixed, k = operands(s, rim_at, rims)
            total = total + fields[pl.ds(k, 1), rim_at : rim_at + rims] * mixed
        for i in range(2 * halves + 1):
            product[tiles + i] = total[:, i * 128 : (i + 1) * 128]

        for r in range(0, width, 8):
            part = slice(r, r + 8)
            tile = [[product[x * halves + h, part, :] for h in range(halves)] for x in range(layers)]
            low = [product[tiles + h, part, :] for h in range(halves)]
            high = [product[tiles + halves + h, part, :] for h in range(halves)]
            rim = product[tiles + 2 * halves, part, :]
            lap = laplacian(tile, low, high, rim, geometry, 8)
            for t in range(tiles):
                row = pl.multiple_of(n * width + r, 8)
                out_ref[t, pl.ds(row, 8), :] = 0.5 * (
                    cross[t, part, :] - lap[t // halves][t % halves]
                )
        return carry

    lax.fori_loop(0, blocks, one_block, 0)


def unpack_kernel(geometry, *rest):
    layers, halves, ny, depth, chips = geometry
    parts, out_ref, stage = rest[:chips], rest[chips], rest[chips + 1]
    me = lax.axis_index("modes") // 2
    for e in range(chips):
        stage[e ^ me] = parts[e][...]
    lanes = lane_index(8)
    modes = out_ref.shape[0] // (layers * ny)

    def group(g, carry):
        source = pl.multiple_of(g * 8, 8)
        for x in range(layers):
            tiles = [
                stage[d // halves, x * halves + d % halves, pl.ds(source, 8), :] for d in range(ny)
            ]
            tiles = swap_lanes(tiles, depth, lanes)
            for y in range(ny):
                out_ref[pl.ds(g * 8 * layers * ny + x * ny + y, 8, stride=layers * ny), :] = tiles[y]
        return carry

    lax.fori_loop(0, modes // 8, group, 0)


def vmem(count):
    return [pl.BlockSpec(memory_space=pltpu.VMEM)] * count


def on_device(solution_modes, coefficient_modes, coupling, source_block, expansion_index):
    local_u, layers, ny, nz = solution_modes.shape
    local_a = coefficient_modes.shape[0]
    blocks, slots, width = coupling.shape[:3]
    count = lax.axis_size("modes")
    chips = count // 2
    depth = 128 // ny
    halves = (nz // depth) // chips
    geometry = (layers, halves, ny, depth, chips)
    tiles = layers * halves
    modes = local_u + local_a
    f32 = jnp.float32

    def call(kernel, shapes, inputs, scratch, limit, name, **more):
        return pl.pallas_call(
            kernel,
            out_shape=shapes,
            in_specs=vmem(inputs),
            out_specs=jax.tree.map(lambda _: pl.BlockSpec(memory_space=pltpu.VMEM), shapes),
            scratch_shapes=scratch,
            compiler_params=pltpu.CompilerParams(vmem_limit_bytes=limit * 1024 * 1024),
            name=name,
            **more,
        )

    sends = call(
        functools.partial(pack_fields, geometry),
        [jax.ShapeDtypeStruct((tiles + 1, modes, 128), f32)] * chips,
        2,
        [pltpu.VMEM((chips, tiles + 1, modes, 128), f32)],
        PACK_LIMIT,
        "pack_fields",
    )(solution_modes.reshape(-1, nz), coefficient_modes.reshape(-1, nz))
    rows = blocks * slots * width // (128 // width)
    pack = call(
        pack_coupling, jax.ShapeDtypeStruct((rows + 8, 128), f32), 3, [], PACK_LIMIT, "pack_coupling"
    )(coupling, source_block, expansion_index)

    def trade(value, e):
        return lax.ppermute(value, "modes", [(i, i ^ (2 * e)) for i in range(count)])

    def sibling(value):
        return lax.ppermute(value, "modes", [(i, i ^ 1) for i in range(count)])

    bodies = [sends[0]] + [trade(sends[e], e) for e in range(1, chips)]
    pack_later = lax.optimization_barrier((pack, bodies[1]))[0] if chips > 1 else pack
    packs = [pack] + [trade(pack_later, e) for e in range(1, chips)]
    n_tiles = lax.axis_size("tiles")
    up = [(i, i + 1) for i in range(n_tiles - 1)]
    down = [(i + 1, i) for i in range(n_tiles - 1)]
    low, high, other_low, other_high = [], [], [], []
    for group in (range(0, chips - 1), range(chips - 1, chips)):
        if not len(group):
            continue
        top = jnp.concatenate([bodies[e][tiles - halves : tiles] for e in group])
        bottom = jnp.concatenate([bodies[e][:halves] for e in group])
        part = jnp.concatenate([lax.ppermute(top, "tiles", up), lax.ppermute(bottom, "tiles", down)])
        other = sibling(part)
        size = len(group) * halves
        for i in range(len(group)):
            here = slice(i * halves, (i + 1) * halves)
            there = slice(size + i * halves, size + (i + 1) * halves)
            low.append(part[here])
            high.append(part[there])
            other_low.append(other[here])
            other_high.append(other[there])
    others = [sibling(body) for body in bodies]

    ncol = 2 * tiles * 128 + (2 * halves + 1) * 128
    n_blocks = count * (local_u // width)
    prepared = ()
    for e in range(chips):
        prepared = call(
            functools.partial(prepare_kernel, geometry, width, local_u, local_a, e),
            (
                jax.ShapeDtypeStruct((n_blocks, 3 * width, ncol), jnp.bfloat16),
                jax.ShapeDtypeStruct((count * local_a, ncol), f32),
            ),
            6 + len(prepared),
            [],
            PREPARE_LIMIT,
            "prepare",
            input_output_aliases={6: 0, 7: 1} if prepared else {},
        )(bodies[e], others[e], low[e], other_low[e], high[e], other_high[e], *prepared)
    sources, fields = prepared

    parts = [None] * chips
    for e in list(range(chips - 1, -1, -1)):
        result = call(
            functools.partial(apply_kernel, geometry, blocks, slots, width),
            jax.ShapeDtypeStruct((tiles, local_u, 128), f32),
            3,
            [
                pltpu.VMEM((rows, 128 // width * 128), jnp.bfloat16),
                pltpu.VMEM((8, 128), jnp.int32),
                pltpu.SMEM((8, 128), jnp.int32),
                pltpu.VMEM((tiles + 2 * halves + 1, width, 128), f32),
                pltpu.VMEM((tiles, width, 128), f32),
                pltpu.SemaphoreType.DMA,
            ],
            APPLY_LIMIT,
            "apply",
        )(packs[e], sources, fields)
        parts[e] = trade(result, e) if e else result
    out = call(
        functools.partial(unpack_kernel, geometry),
        jax.ShapeDtypeStruct((local_u * layers * ny, nz), f32),
        chips,
        [pltpu.VMEM((chips, tiles, local_u, 128), f32)],
        PACK_LIMIT,
        "unpack",
    )(*parts)
    return out.reshape(solution_modes.shape)


def solution(mesh):
    placed = (
        P("modes", "tiles", None, None),
        P("modes", "tiles", None, None),
        P("modes", None, None, None),
        P("modes", None),
        P("modes", None),
    )
    return jax.shard_map(
        on_device,
        mesh=mesh,
        in_specs=placed,
        out_specs=P("modes", "tiles", None, None),
        check_vma=False,
    )
```

```python
import functools

import jax
import jax.numpy as jnp
from jax import lax
from jax.experimental import pallas as pl
from jax.experimental.pallas import tpu as pltpu
from jax.sharding import PartitionSpec as P

PACK_LIMIT = 60
PREPARE_LIMIT = 24
UNPACK_LIMIT = 16
APPLY_LIMIT = 24
CHUNK = 4
PIECES = 4


def lane_index(rows):
    return lax.broadcasted_iota(jnp.int32, (rows, 128), 1)


def swap_lanes(tiles, depth, lanes):
    tiles = list(tiles)
    size = len(tiles)
    step = 1
    while step < size:
        width = step * depth
        upper = (lanes & width) != 0
        for low in range(size):
            if low & step:
                continue
            high = low | step
            first, second = tiles[low], tiles[high]
            tiles[low] = jnp.where(upper, pltpu.roll(second, width, 1), first)
            tiles[high] = jnp.where(upper, second, pltpu.roll(first, 128 - width, 1))
        step *= 2
    return tiles


def turn(value, shift):
    shift = shift % 128
    return value if shift == 0 else pltpu.roll(value, shift, 1)


def pack_kernel(geometry, u_hbm, a_hbm, coupling_hbm, source_hbm, expansion_hbm, *rest):
    layers, halves, ny, depth, chips = geometry
    sends, pack = rest[:chips], rest[chips]
    stage, u_ref, a_ref, coupling_ref, source_ref, expansion_ref, sems = rest[chips + 1 :]
    me = lax.axis_index("modes") // 2
    rows_u = u_ref.shape[0] // PIECES
    pairs = [(a_hbm, a_ref)]
    pairs += [(u_hbm.at[pl.ds(i * rows_u, rows_u)], u_ref.at[pl.ds(i * rows_u, rows_u)]) for i in range(PIECES)]
    pairs += [(coupling_hbm, coupling_ref), (source_hbm, source_ref), (expansion_hbm, expansion_ref)]
    copies = [pltpu.make_async_copy(one, two, sems.at[i]) for i, (one, two) in enumerate(pairs)]
    for copy in copies:
        copy.start()
    lanes = lane_index(8)
    place = lanes % depth
    cells = layers * ny

    def regroup(ref, first, count, target):
        def group(g, carry):
            to = pl.multiple_of(target + g * 8, 8)
            by_layer = []
            for x in range(layers):
                tiles = [ref[pl.ds((first + g * 8) * cells + x * ny + y, 8, stride=cells), :] for y in range(ny)]
                tiles = swap_lanes(tiles, depth, lanes)
                by_layer.append(tiles)
                for d in range(ny):
                    stage[d // halves, x * halves + d % halves, pl.ds(to, 8), :] = tiles[d]
            for chip in range(chips):
                rim = jnp.zeros((8, 128), jnp.float32)
                left, right = chip * halves - 1, (chip + 1) * halves
                for x in range(layers):
                    if left >= 0:
                        rim = jnp.where(place == x, turn(by_layer[x][left], x + 1 - depth), rim)
                    if right < ny:
                        at = depth // 2 + x
                        rim = jnp.where(place == at, turn(by_layer[x][right], at), rim)
                stage[chip, layers * halves, pl.ds(to, 8), :] = rim
            return carry

        lax.fori_loop(0, count // 8, group, 0, unroll=True)
        for e in range(chips):
            rows = pl.ds(target, count)
            copy = pltpu.make_async_copy(
                stage.at[e ^ me, :, rows], sends[e].at[:, rows], sems.at[len(copies) + len(sent)]
            )
            copy.start()
            sent.append(copy)

    sent = []
    local_a, local_u = a_ref.shape[0] // cells, u_ref.shape[0] // cells
    copies[0].wait()
    regroup(a_ref, 0, local_a, local_u)
    for i in range(PIECES):
        copies[1 + i].wait()
        regroup(u_ref, i * (local_u // PIECES), local_u // PIECES, i * (local_u // PIECES))
    for copy in copies[1 + PIECES :]:
        copy.wait()
    blocks, slots, width, _ = coupling_ref.shape
    per = 128 // width
    groups = slots // per
    for block in range(blocks):
        for g in range(groups):
            rows = slice((block * groups + g) * width, (block * groups + g + 1) * width)
            pack[rows, :] = jnp.concatenate(
                [coupling_ref[block, g * per + q] for q in range(per)], axis=1
            )
    last = blocks * groups * width
    pack[last : last + 8, :] = jnp.zeros((8, 128), jnp.float32)
    pack[last : last + blocks, 0:slots] = source_ref[...].astype(jnp.float32)
    pack[last + blocks : last + 2 * blocks, 0:slots] = expansion_ref[...].astype(jnp.float32)
    for copy in sent:
        copy.wait()


def laplacian(tile, low, high, rim, geometry, rows):
    layers, halves, ny, depth, _ = geometry
    lanes = lane_index(rows)
    place = lanes % depth
    first_row, last_row = lanes < depth, lanes >= 128 - depth
    result = []
    for x in range(layers):
        result.append([])
        for h in range(halves):
            c = tile[x][h]
            before = tile[x - 1][h] if x else low[h]
            after = tile[x + 1][h] if x + 1 < layers else high[h]
            up = jnp.where(first_row, 0.0, turn(c, depth))
            down = jnp.where(last_row, 0.0, turn(c, -depth))
            edge = turn(tile[x][h - 1], 1 - depth) if h else turn(rim, -x)
            left = jnp.where(place == 0, edge, turn(c, 1))
            if h + 1 < halves:
                edge = turn(tile[x][h + 1], depth - 1)
            else:
                edge = turn(rim, depth - 1 - depth // 2 - x)
            right = jnp.where(place == depth - 1, edge, turn(c, -1))
            result[-1].append(((before + after) + (up + down)) + ((left + right) - 6.0 * c))
    return result


def halves_of(value):
    upper = value.astype(jnp.bfloat16)
    lower = (value - upper.astype(jnp.float32)).astype(jnp.bfloat16)
    return upper, lower


def columns(tile, tiles):
    base = (tile // CHUNK) * 2 * CHUNK * 128 + (tile % CHUNK) * 128
    return base, base + CHUNK * 128


def prepare_kernel(geometry, width, local_u, local_a, group, *rest):
    layers, halves, ny, depth, chips = geometry
    many = len(group)
    bodies, low_ref, high_ref, other = rest[:many], rest[many], rest[many + 1], rest[many + 2]
    sources, fields = rest[-2:]
    tiles = layers * halves
    rim_at = 2 * tiles * 128
    me = lax.axis_index("modes")

    for i, side in [(i, side) for i in range(many) for side in range(2)]:
        first = i * (tiles + 1)
        body = other.at[pl.ds(first, tiles + 1)] if side else bodies[i]
        first = many * (tiles + 1) + i * halves
        low = other.at[pl.ds(first, halves)] if side else low_ref.at[pl.ds(i * halves, halves)]
        first += many * halves
        high = other.at[pl.ds(first, halves)] if side else high_ref.at[pl.ds(i * halves, halves)]
        device = me ^ (2 * group[i]) ^ side

        def load(start, rows, body=body, low=low, high=high):
            part = pl.ds(start, rows)
            tile = [[body[x * halves + h, part, :] for h in range(halves)] for x in range(layers)]
            below = [low[h, part, :] for h in range(halves)]
            above = [high[h, part, :] for h in range(halves)]
            return tile, below, above, body[tiles, part, :]

        def prepare_u(g, carry, load=load, device=device):
            start = pl.multiple_of(g * 16, 16)
            tile, below, above, rim = load(start, 16)
            lap = laplacian(tile, below, above, rim, geometry, 16)
            block = device * (local_u // width) + (g * 16) // width
            row = pl.multiple_of((g * 16) % width, 16)

            def put(value, at):
                upper, lower = halves_of(value)
                where = pl.ds(at, 128)
                sources[block, pl.ds(row, 16), where] = upper
                sources[block, pl.ds(width + row, 16), where] = lower
                sources[block, pl.ds(2 * width + row, 16), where] = upper

            for t in range(tiles):
                x, h = t // halves, t % halves
                put(tile[x][h], columns(t, tiles)[0])
                put(lap[x][h], columns(t, tiles)[1])
            for h in range(halves):
                put(below[h], rim_at + h * 128)
                put(above[h], rim_at + (halves + h) * 128)
            put(rim, rim_at + 2 * halves * 128)
            return carry

        lax.fori_loop(0, local_u // 16, prepare_u, 0, unroll=4)
        tile, below, above, rim = load(local_u, local_a)
        lap = laplacian(tile, below, above, rim, geometry, local_a)
        rows = pl.ds(pl.multiple_of(device * local_a, local_a), local_a)
        for t in range(tiles):
            x, h = t // halves, t % halves
            fields[rows, pl.ds(columns(t, tiles)[0], 128)] = tile[x][h]
            fields[rows, pl.ds(columns(t, tiles)[1], 128)] = lap[x][h]
        for h in range(halves):
            fields[rows, pl.ds(rim_at + h * 128, 128)] = below[h]
            fields[rows, pl.ds(rim_at + (halves + h) * 128, 128)] = above[h]
        fields[rows, pl.ds(rim_at + 2 * halves * 128, 128)] = rim


def apply_kernel(geometry, blocks, slots, width, pack, sources, fields, out_ref, mix, numbers, table, product, cross, sem):
    layers, halves, ny, depth, chips = geometry
    tiles = layers * halves
    chunks = tiles // CHUNK
    span = CHUNK * 128
    rim_at = 2 * tiles * 128
    rims = (2 * halves + 1) * 128
    per = 128 // width
    rows = blocks * slots // per * width

    numbers[...] = pack[rows : rows + 8, :].astype(jnp.int32)
    copy = pltpu.make_async_copy(numbers, table, sem)
    copy.start()
    value = pack[0:rows, :]
    upper, lower = halves_of(value)
    take = lax.broadcasted_iota(jnp.int32, (256, per * 128), 0)
    give = lax.broadcasted_iota(jnp.int32, (256, per * 128), 1)
    lane = give % 128
    wanted = (give // 128) * width + lane % width + jnp.where(lane >= 2 * width, 128, 0)
    chosen = jnp.where((take == wanted) & (lane < 3 * width), 1.0, 0.0).astype(jnp.bfloat16)
    mix[...] = jnp.dot(
        jnp.concatenate([upper, lower], axis=1), chosen, preferred_element_type=jnp.float32
    ).astype(jnp.bfloat16)
    copy.wait()

    def one_block(n, carry):
        def operands(s, first, count):
            j, k = table[n, s], table[blocks + n, s]
            group = pl.multiple_of((n * (slots // per) + s // per) * width, width)
            lanes = (s % per) * 128
            mixed = jnp.dot(
                mix[pl.ds(group, width), lanes : lanes + 3 * width],
                sources[j, :, first : first + count],
                preferred_element_type=jnp.float32,
            )
            return mixed, k

        for chunk in range(chunks):
            base = chunk * 2 * span
            total = jnp.zeros((width, span), jnp.float32)
            rest_total = jnp.zeros((width, span), jnp.float32)
            for s in range(slots):
                mixed, k = operands(s, base, 2 * span)
                field = fields[pl.ds(k, 1), base : base + span]
                bent = fields[pl.ds(k, 1), base + span : base + 2 * span]
                value, curve = mixed[:, :span], mixed[:, span:]
                total = total + field * value
                rest_total = rest_total + (bent * value - field * curve)
            for i in range(CHUNK):
                product[chunk * CHUNK + i] = total[:, i * 128 : (i + 1) * 128]
                cross[chunk * CHUNK + i] = rest_total[:, i * 128 : (i + 1) * 128]

        total = jnp.zeros((width, rims), jnp.float32)
        for s in range(slots):
            mixed, k = operands(s, rim_at, rims)
            total = total + fields[pl.ds(k, 1), rim_at : rim_at + rims] * mixed
        for i in range(2 * halves + 1):
            product[tiles + i] = total[:, i * 128 : (i + 1) * 128]

        for r in range(0, width, 8):
            part = slice(r, r + 8)
            tile = [[product[x * halves + h, part, :] for h in range(halves)] for x in range(layers)]
            low = [product[tiles + h, part, :] for h in range(halves)]
            high = [product[tiles + halves + h, part, :] for h in range(halves)]
            rim = product[tiles + 2 * halves, part, :]
            lap = laplacian(tile, low, high, rim, geometry, 8)
            for t in range(tiles):
                row = pl.multiple_of(n * width + r, 8)
                out_ref[t, pl.ds(row, 8), :] = 0.5 * (
                    cross[t, part, :] - lap[t // halves][t % halves]
                )
        return carry

    lax.fori_loop(0, blocks, one_block, 0)


def unpack_kernel(geometry, *rest):
    layers, halves, ny, depth, chips = geometry
    parts, out_hbm = rest[:chips], rest[chips]
    stage, out_ref, sems = rest[chips + 1 :]
    me = lax.axis_index("modes") // 2
    for e in range(chips):
        stage[e ^ me] = parts[e][...]
    lanes = lane_index(8)
    cells = layers * ny
    modes = out_ref.shape[0] // cells
    size = modes // PIECES

    def group(g, carry):
        source = pl.multiple_of(g * 8, 8)
        for x in range(layers):
            tiles = [stage[d // halves, x * halves + d % halves, pl.ds(source, 8), :] for d in range(ny)]
            tiles = swap_lanes(tiles, depth, lanes)
            for y in range(ny):
                out_ref[pl.ds(g * 8 * cells + x * ny + y, 8, stride=cells), :] = tiles[y]
        return carry

    copies = []
    for i in range(PIECES):
        lax.fori_loop(i * size // 8, (i + 1) * size // 8, group, 0)
        rows = pl.ds(i * size * cells, size * cells)
        copies.append(pltpu.make_async_copy(out_ref.at[rows], out_hbm.at[rows], sems.at[i]))
        copies[-1].start()
    for copy in copies:
        copy.wait()


def vmem(count):
    return [pl.BlockSpec(memory_space=pltpu.VMEM)] * count


def on_device(solution_modes, coefficient_modes, coupling, source_block, expansion_index):
    local_u, layers, ny, nz = solution_modes.shape
    local_a = coefficient_modes.shape[0]
    blocks, slots, width = coupling.shape[:3]
    count = lax.axis_size("modes")
    chips = count // 2
    depth = 128 // ny
    halves = (nz // depth) // chips
    geometry = (layers, halves, ny, depth, chips)
    tiles = layers * halves
    modes = local_u + local_a
    f32 = jnp.float32

    def call(kernel, shapes, inputs, scratch, limit, name, **more):
        return pl.pallas_call(
            kernel,
            out_shape=shapes,
            in_specs=vmem(inputs),
            out_specs=jax.tree.map(lambda _: pl.BlockSpec(memory_space=pltpu.VMEM), shapes),
            scratch_shapes=scratch,
            compiler_params=pltpu.CompilerParams(vmem_limit_bytes=limit * 1024 * 1024),
            name=name,
            **more,
        )

    rows = blocks * slots * width // (128 // width)
    *sends, pack = pl.pallas_call(
        functools.partial(pack_kernel, geometry),
        out_shape=[jax.ShapeDtypeStruct((tiles + 1, modes, 128), f32)] * chips
        + [jax.ShapeDtypeStruct((rows + 8, 128), f32)],
        in_specs=[pl.BlockSpec(memory_space=pltpu.HBM)] * 5,
        out_specs=[pl.BlockSpec(memory_space=pltpu.HBM)] * chips + vmem(1),
        scratch_shapes=[
            pltpu.VMEM((chips, tiles + 1, modes, 128), f32),
            pltpu.VMEM((local_u * layers * ny, nz), f32),
            pltpu.VMEM((local_a * layers * ny, nz), f32),
            pltpu.VMEM(coupling.shape, f32),
            pltpu.VMEM(source_block.shape, jnp.int32),
            pltpu.VMEM(expansion_index.shape, jnp.int32),
            pltpu.SemaphoreType.DMA((PIECES + 4 + chips * (PIECES + 1),)),
        ],
        compiler_params=pltpu.CompilerParams(vmem_limit_bytes=PACK_LIMIT * 1024 * 1024),
        name="pack",
    )(
        solution_modes.reshape(-1, nz),
        coefficient_modes.reshape(-1, nz),
        coupling,
        source_block,
        expansion_index,
    )

    def trade(value, e):
        return lax.ppermute(value, "modes", [(i, i ^ (2 * e)) for i in range(count)])

    def sibling(value):
        return lax.ppermute(value, "modes", [(i, i ^ 1) for i in range(count)])

    bodies = [sends[0]] + [trade(sends[e], e) for e in range(1, chips)]
    late = lax.optimization_barrier((pack, bodies[-1]))[0]
    packs = [pack] + [trade(late, e) for e in range(1, chips)]
    n_tiles = lax.axis_size("tiles")
    up = [(i, i + 1) for i in range(n_tiles - 1)]
    down = [(i + 1, i) for i in range(n_tiles - 1)]
    gathered = []
    for group in (range(0, chips // 2), range(chips // 2, chips)):
        top = jnp.concatenate([bodies[e][tiles - halves : tiles] for e in group])
        bottom = jnp.concatenate([bodies[e][:halves] for e in group])
        low, high = lax.ppermute(top, "tiles", up), lax.ppermute(bottom, "tiles", down)
        mine = [bodies[e] for e in group] + [low, high]
        gathered.append((group, mine + [sibling(jnp.concatenate(mine))]))

    ncol = 2 * tiles * 128 + (2 * halves + 1) * 128
    n_blocks = count * (local_u // width)
    prepared = ()
    for group, inputs in gathered:
        prepared = call(
            functools.partial(prepare_kernel, geometry, width, local_u, local_a, group),
            (
                jax.ShapeDtypeStruct((n_blocks, 3 * width, ncol), jnp.bfloat16),
                jax.ShapeDtypeStruct((count * local_a, ncol), f32),
            ),
            len(inputs) + len(prepared),
            [],
            PREPARE_LIMIT,
            "prepare",
            input_output_aliases={len(inputs): 0, len(inputs) + 1: 1} if prepared else {},
        )(*inputs, *prepared)
    sources, fields = prepared

    parts = [None] * chips
    for e in list(range(chips - 1, -1, -1)):
        result = call(
            functools.partial(apply_kernel, geometry, blocks, slots, width),
            jax.ShapeDtypeStruct((tiles, local_u, 128), f32),
            3,
            [
                pltpu.VMEM((rows, 128 // width * 128), jnp.bfloat16),
                pltpu.VMEM((8, 128), jnp.int32),
                pltpu.SMEM((8, 128), jnp.int32),
                pltpu.VMEM((tiles + 2 * halves + 1, width, 128), f32),
                pltpu.VMEM((tiles, width, 128), f32),
                pltpu.SemaphoreType.DMA,
            ],
            APPLY_LIMIT,
            "apply",
        )(packs[e], sources, fields)
        parts[e] = trade(result, e) if e else result
    out = pl.pallas_call(
        functools.partial(unpack_kernel, geometry),
        out_shape=jax.ShapeDtypeStruct((local_u * layers * ny, nz), f32),
        in_specs=vmem(chips),
        out_specs=pl.BlockSpec(memory_space=pl.ANY),
        scratch_shapes=[
            pltpu.VMEM((chips, tiles, local_u, 128), f32),
            pltpu.VMEM((local_u * layers * ny, nz), f32),
            pltpu.SemaphoreType.DMA((PIECES,)),
        ],
        compiler_params=pltpu.CompilerParams(vmem_limit_bytes=UNPACK_LIMIT * 1024 * 1024),
        name="unpack",
    )(*parts)
    return out.reshape(solution_modes.shape)


def solution(mesh):
    placed = (
        P("modes", "tiles", None, None),
        P("modes", "tiles", None, None),
        P("modes", None, None, None),
        P("modes", None),
        P("modes", None),
    )
    return jax.shard_map(
        on_device,
        mesh=mesh,
        in_specs=placed,
        out_specs=P("modes", "tiles", None, None),
        check_vma=False,
    )
```

```python
import functools

import jax
import jax.numpy as jnp
from jax import lax
from jax.experimental import pallas as pl
from jax.experimental.pallas import tpu as pltpu
from jax.sharding import PartitionSpec as P

PACK_LIMIT = 60
PREPARE_LIMIT = 24
UNPACK_LIMIT = 16
APPLY_LIMIT = 24
CHUNK = 4
PIECES = 4


def lane_index(rows):
    return lax.broadcasted_iota(jnp.int32, (rows, 128), 1)


def swap_lanes(tiles, depth, lanes):
    tiles = list(tiles)
    size = len(tiles)
    step = 1
    while step < size:
        width = step * depth
        upper = (lanes & width) != 0
        for low in range(size):
            if low & step:
                continue
            high = low | step
            first, second = tiles[low], tiles[high]
            tiles[low] = jnp.where(upper, pltpu.roll(second, width, 1), first)
            tiles[high] = jnp.where(upper, second, pltpu.roll(first, 128 - width, 1))
        step *= 2
    return tiles


def turn(value, shift):
    shift = shift % 128
    return value if shift == 0 else pltpu.roll(value, shift, 1)


def pack_kernel(geometry, u_hbm, a_hbm, *rest):
    layers, halves, ny, depth, chips = geometry
    sends, (stage, u_ref, a_ref, sems) = rest[:chips], rest[chips:]
    me = lax.axis_index("modes") // 2
    rows_u = u_ref.shape[0] // PIECES
    pairs = [(a_hbm, a_ref)]
    pairs += [(u_hbm.at[pl.ds(i * rows_u, rows_u)], u_ref.at[pl.ds(i * rows_u, rows_u)]) for i in range(PIECES)]
    copies = [pltpu.make_async_copy(one, two, sems.at[i]) for i, (one, two) in enumerate(pairs)]
    for copy in copies:
        copy.start()
    lanes = lane_index(8)
    place = lanes % depth
    cells = layers * ny

    def regroup(ref, first, count, target):
        def group(g, carry):
            to = pl.multiple_of(target + g * 8, 8)
            by_layer = []
            for x in range(layers):
                tiles = [ref[pl.ds((first + g * 8) * cells + x * ny + y, 8, stride=cells), :] for y in range(ny)]
                tiles = swap_lanes(tiles, depth, lanes)
                by_layer.append(tiles)
                for d in range(ny):
                    stage[d // halves, x * halves + d % halves, pl.ds(to, 8), :] = tiles[d]
            for chip in range(chips):
                rim = jnp.zeros((8, 128), jnp.float32)
                left, right = chip * halves - 1, (chip + 1) * halves
                for x in range(layers):
                    if left >= 0:
                        rim = jnp.where(place == x, turn(by_layer[x][left], x + 1 - depth), rim)
                    if right < ny:
                        at = depth // 2 + x
                        rim = jnp.where(place == at, turn(by_layer[x][right], at), rim)
                stage[chip, layers * halves, pl.ds(to, 8), :] = rim
            return carry

        lax.fori_loop(0, count // 8, group, 0, unroll=True)
        for e in range(chips):
            rows = pl.ds(target, count)
            copy = pltpu.make_async_copy(
                stage.at[e ^ me, :, rows], sends[e].at[:, rows], sems.at[len(copies) + len(sent)]
            )
            copy.start()
            sent.append(copy)

    sent = []
    local_a, local_u = a_ref.shape[0] // cells, u_ref.shape[0] // cells
    copies[0].wait()
    regroup(a_ref, 0, local_a, local_u)
    for i in range(PIECES):
        copies[1 + i].wait()
        regroup(u_ref, i * (local_u // PIECES), local_u // PIECES, i * (local_u // PIECES))
    for copy in sent:
        copy.wait()


def pack_coupling(coupling_ref, source_ref, expansion_ref, pack):
    blocks, slots, width, _ = coupling_ref.shape
    per = 128 // width
    groups = slots // per
    for block in range(blocks):
        for g in range(groups):
            rows = slice((block * groups + g) * width, (block * groups + g + 1) * width)
            pack[rows, :] = jnp.concatenate(
                [coupling_ref[block, g * per + q] for q in range(per)], axis=1
            )
    last = blocks * groups * width
    pack[last : last + 8, :] = jnp.zeros((8, 128), jnp.float32)
    pack[last : last + blocks, 0:slots] = source_ref[...].astype(jnp.float32)
    pack[last + blocks : last + 2 * blocks, 0:slots] = expansion_ref[...].astype(jnp.float32)


def laplacian(tile, low, high, rim, geometry, rows):
    layers, halves, ny, depth, _ = geometry
    lanes = lane_index(rows)
    place = lanes % depth
    first_row, last_row = lanes < depth, lanes >= 128 - depth
    result = []
    for x in range(layers):
        result.append([])
        for h in range(halves):
            c = tile[x][h]
            before = tile[x - 1][h] if x else low[h]
            after = tile[x + 1][h] if x + 1 < layers else high[h]
            up = jnp.where(first_row, 0.0, turn(c, depth))
            down = jnp.where(last_row, 0.0, turn(c, -depth))
            edge = turn(tile[x][h - 1], 1 - depth) if h else turn(rim, -x)
            left = jnp.where(place == 0, edge, turn(c, 1))
            if h + 1 < halves:
                edge = turn(tile[x][h + 1], depth - 1)
            else:
                edge = turn(rim, depth - 1 - depth // 2 - x)
            right = jnp.where(place == depth - 1, edge, turn(c, -1))
            result[-1].append(((before + after) + (up + down)) + ((left + right) - 6.0 * c))
    return result


def halves_of(value):
    upper = value.astype(jnp.bfloat16)
    lower = (value - upper.astype(jnp.float32)).astype(jnp.bfloat16)
    return upper, lower


def columns(tile, tiles):
    base = (tile // CHUNK) * 2 * CHUNK * 128 + (tile % CHUNK) * 128
    return base, base + CHUNK * 128


def prepare_kernel(geometry, width, local_u, local_a, group, *rest):
    layers, halves, ny, depth, chips = geometry
    many = len(group)
    bodies, low_ref, high_ref, other = rest[:many], rest[many], rest[many + 1], rest[many + 2]
    sources, fields = rest[-2:]
    tiles = layers * halves
    rim_at = 2 * tiles * 128
    me = lax.axis_index("modes")

    for i, side in [(i, side) for i in range(many) for side in range(2)]:
        first = i * (tiles + 1)
        body = other.at[pl.ds(first, tiles + 1)] if side else bodies[i]
        first = many * (tiles + 1) + i * halves
        low = other.at[pl.ds(first, halves)] if side else low_ref.at[pl.ds(i * halves, halves)]
        first += many * halves
        high = other.at[pl.ds(first, halves)] if side else high_ref.at[pl.ds(i * halves, halves)]
        device = me ^ (2 * group[i]) ^ side

        def load(start, rows, body=body, low=low, high=high):
            part = pl.ds(start, rows)
            tile = [[body[x * halves + h, part, :] for h in range(halves)] for x in range(layers)]
            below = [low[h, part, :] for h in range(halves)]
            above = [high[h, part, :] for h in range(halves)]
            return tile, below, above, body[tiles, part, :]

        def prepare_u(g, carry, load=load, device=device):
            start = pl.multiple_of(g * 16, 16)
            tile, below, above, rim = load(start, 16)
            lap = laplacian(tile, below, above, rim, geometry, 16)
            block = device * (local_u // width) + (g * 16) // width
            row = pl.multiple_of((g * 16) % width, 16)

            def put(value, at):
                upper, lower = halves_of(value)
                where = pl.ds(at, 128)
                sources[block, pl.ds(row, 16), where] = upper
                sources[block, pl.ds(width + row, 16), where] = lower
                sources[block, pl.ds(2 * width + row, 16), where] = upper

            for t in range(tiles):
                x, h = t // halves, t % halves
                put(tile[x][h], columns(t, tiles)[0])
                put(lap[x][h], columns(t, tiles)[1])
            for h in range(halves):
                put(below[h], rim_at + h * 128)
                put(above[h], rim_at + (halves + h) * 128)
            put(rim, rim_at + 2 * halves * 128)
            return carry

        lax.fori_loop(0, local_u // 16, prepare_u, 0, unroll=4)
        tile, below, above, rim = load(local_u, local_a)
        lap = laplacian(tile, below, above, rim, geometry, local_a)
        rows = pl.ds(pl.multiple_of(device * local_a, local_a), local_a)
        for t in range(tiles):
            x, h = t // halves, t % halves
            fields[rows, pl.ds(columns(t, tiles)[0], 128)] = tile[x][h]
            fields[rows, pl.ds(columns(t, tiles)[1], 128)] = lap[x][h]
        for h in range(halves):
            fields[rows, pl.ds(rim_at + h * 128, 128)] = below[h]
            fields[rows, pl.ds(rim_at + (halves + h) * 128, 128)] = above[h]
        fields[rows, pl.ds(rim_at + 2 * halves * 128, 128)] = rim


def apply_kernel(geometry, blocks, slots, width, pack, sources, fields, out_ref, mix, numbers, table, product, cross, sem):
    layers, halves, ny, depth, chips = geometry
    tiles = layers * halves
    chunks = tiles // CHUNK
    span = CHUNK * 128
    rim_at = 2 * tiles * 128
    rims = (2 * halves + 1) * 128
    per = 128 // width
    rows = blocks * slots // per * width

    numbers[...] = pack[rows : rows + 8, :].astype(jnp.int32)
    copy = pltpu.make_async_copy(numbers, table, sem)
    copy.start()
    value = pack[0:rows, :]
    upper, lower = halves_of(value)
    take = lax.broadcasted_iota(jnp.int32, (256, per * 128), 0)
    give = lax.broadcasted_iota(jnp.int32, (256, per * 128), 1)
    lane = give % 128
    wanted = (give // 128) * width + lane % width + jnp.where(lane >= 2 * width, 128, 0)
    chosen = jnp.where((take == wanted) & (lane < 3 * width), 1.0, 0.0).astype(jnp.bfloat16)
    mix[...] = jnp.dot(
        jnp.concatenate([upper, lower], axis=1), chosen, preferred_element_type=jnp.float32
    ).astype(jnp.bfloat16)
    copy.wait()

    def one_block(n, carry):
        def operands(s, first, count):
            j, k = table[n, s], table[blocks + n, s]
            group = pl.multiple_of((n * (slots // per) + s // per) * width, width)
            lanes = (s % per) * 128
            mixed = jnp.dot(
                mix[pl.ds(group, width), lanes : lanes + 3 * width],
                sources[j, :, first : first + count],
                preferred_element_type=jnp.float32,
            )
            return mixed, k

        for chunk in range(chunks):
            base = chunk * 2 * span
            total = jnp.zeros((width, span), jnp.float32)
            rest_total = jnp.zeros((width, span), jnp.float32)
            for s in range(slots):
                mixed, k = operands(s, base, 2 * span)
                field = fields[pl.ds(k, 1), base : base + span]
                bent = fields[pl.ds(k, 1), base + span : base + 2 * span]
                value, curve = mixed[:, :span], mixed[:, span:]
                total = total + field * value
                rest_total = rest_total + (bent * value - field * curve)
            for i in range(CHUNK):
                product[chunk * CHUNK + i] = total[:, i * 128 : (i + 1) * 128]
                cross[chunk * CHUNK + i] = rest_total[:, i * 128 : (i + 1) * 128]

        total = jnp.zeros((width, rims), jnp.float32)
        for s in range(slots):
            mixed, k = operands(s, rim_at, rims)
            total = total + fields[pl.ds(k, 1), rim_at : rim_at + rims] * mixed
        for i in range(2 * halves + 1):
            product[tiles + i] = total[:, i * 128 : (i + 1) * 128]

        for r in range(0, width, 8):
            part = slice(r, r + 8)
            tile = [[product[x * halves + h, part, :] for h in range(halves)] for x in range(layers)]
            low = [product[tiles + h, part, :] for h in range(halves)]
            high = [product[tiles + halves + h, part, :] for h in range(halves)]
            rim = product[tiles + 2 * halves, part, :]
            lap = laplacian(tile, low, high, rim, geometry, 8)
            for t in range(tiles):
                row = pl.multiple_of(n * width + r, 8)
                out_ref[t, pl.ds(row, 8), :] = 0.5 * (
                    cross[t, part, :] - lap[t // halves][t % halves]
                )
        return carry

    lax.fori_loop(0, blocks, one_block, 0)


def unpack_kernel(geometry, *rest):
    layers, halves, ny, depth, chips = geometry
    parts, out_hbm = rest[:chips], rest[chips]
    stage, out_ref, sems = rest[chips + 1 :]
    me = lax.axis_index("modes") // 2
    for e in range(chips):
        stage[e ^ me] = parts[e][...]
    lanes = lane_index(8)
    cells = layers * ny
    modes = out_ref.shape[0] // cells
    size = modes // PIECES

    def group(g, carry):
        source = pl.multiple_of(g * 8, 8)
        for x in range(layers):
            tiles = [stage[d // halves, x * halves + d % halves, pl.ds(source, 8), :] for d in range(ny)]
            tiles = swap_lanes(tiles, depth, lanes)
            for y in range(ny):
                out_ref[pl.ds(g * 8 * cells + x * ny + y, 8, stride=cells), :] = tiles[y]
        return carry

    copies = []
    for i in range(PIECES):
        lax.fori_loop(i * size // 8, (i + 1) * size // 8, group, 0)
        rows = pl.ds(i * size * cells, size * cells)
        copies.append(pltpu.make_async_copy(out_ref.at[rows], out_hbm.at[rows], sems.at[i]))
        copies[-1].start()
    for copy in copies:
        copy.wait()


def vmem(count):
    return [pl.BlockSpec(memory_space=pltpu.VMEM)] * count


def on_device(solution_modes, coefficient_modes, coupling, source_block, expansion_index):
    local_u, layers, ny, nz = solution_modes.shape
    local_a = coefficient_modes.shape[0]
    blocks, slots, width = coupling.shape[:3]
    count = lax.axis_size("modes")
    chips = count // 2
    depth = 128 // ny
    halves = (nz // depth) // chips
    geometry = (layers, halves, ny, depth, chips)
    tiles = layers * halves
    modes = local_u + local_a
    f32 = jnp.float32

    def call(kernel, shapes, inputs, scratch, limit, name, **more):
        return pl.pallas_call(
            kernel,
            out_shape=shapes,
            in_specs=vmem(inputs),
            out_specs=jax.tree.map(lambda _: pl.BlockSpec(memory_space=pltpu.VMEM), shapes),
            scratch_shapes=scratch,
            compiler_params=pltpu.CompilerParams(vmem_limit_bytes=limit * 1024 * 1024),
            name=name,
            **more,
        )

    rows = blocks * slots * width // (128 // width)
    sends = pl.pallas_call(
        functools.partial(pack_kernel, geometry),
        out_shape=[jax.ShapeDtypeStruct((tiles + 1, modes, 128), f32)] * chips,
        in_specs=[pl.BlockSpec(memory_space=pltpu.HBM)] * 2,
        out_specs=[pl.BlockSpec(memory_space=pltpu.HBM)] * chips,
        scratch_shapes=[
            pltpu.VMEM((chips, tiles + 1, modes, 128), f32),
            pltpu.VMEM((local_u * layers * ny, nz), f32),
            pltpu.VMEM((local_a * layers * ny, nz), f32),
            pltpu.SemaphoreType.DMA((PIECES + 1 + chips * (PIECES + 1),)),
        ],
        compiler_params=pltpu.CompilerParams(vmem_limit_bytes=PACK_LIMIT * 1024 * 1024),
        name="pack",
    )(
        solution_modes.reshape(-1, nz),
        coefficient_modes.reshape(-1, nz),
    )
    pack = call(
        pack_coupling,
        jax.ShapeDtypeStruct((rows + 8, 128), f32),
        3,
        [],
        UNPACK_LIMIT,
        "pack_coupling",
    )(coupling, source_block, expansion_index)

    def trade(value, e):
        return lax.ppermute(value, "modes", [(i, i ^ (2 * e)) for i in range(count)])

    def sibling(value):
        return lax.ppermute(value, "modes", [(i, i ^ 1) for i in range(count)])

    bodies = [sends[0]] + [trade(sends[e], e) for e in range(1, chips)]
    late = lax.optimization_barrier((pack, bodies[-1]))[0]
    packs = [pack] + [trade(late, e) for e in range(1, chips)]
    n_tiles = lax.axis_size("tiles")
    up = [(i, i + 1) for i in range(n_tiles - 1)]
    down = [(i + 1, i) for i in range(n_tiles - 1)]
    gathered = []
    for group in ([0, chips - 1], list(range(1, chips - 1))):
        top = jnp.concatenate([bodies[e][tiles - halves : tiles] for e in group])
        bottom = jnp.concatenate([bodies[e][:halves] for e in group])
        low, high = lax.ppermute(top, "tiles", up), lax.ppermute(bottom, "tiles", down)
        mine = [bodies[e] for e in group] + [low, high]
        gathered.append((group, mine + [sibling(jnp.concatenate(mine))]))

    ncol = 2 * tiles * 128 + (2 * halves + 1) * 128
    n_blocks = count * (local_u // width)
    prepared = ()
    for group, inputs in gathered:
        prepared = call(
            functools.partial(prepare_kernel, geometry, width, local_u, local_a, group),
            (
                jax.ShapeDtypeStruct((n_blocks, 3 * width, ncol), jnp.bfloat16),
                jax.ShapeDtypeStruct((count * local_a, ncol), f32),
            ),
            len(inputs) + len(prepared),
            [],
            PREPARE_LIMIT,
            "prepare",
            input_output_aliases={len(inputs): 0, len(inputs) + 1: 1} if prepared else {},
        )(*inputs, *prepared)
    sources, fields = prepared

    parts = [None] * chips
    for e in list(range(chips - 1, -1, -1)):
        result = call(
            functools.partial(apply_kernel, geometry, blocks, slots, width),
            jax.ShapeDtypeStruct((tiles, local_u, 128), f32),
            3,
            [
                pltpu.VMEM((rows, 128 // width * 128), jnp.bfloat16),
                pltpu.VMEM((8, 128), jnp.int32),
                pltpu.SMEM((8, 128), jnp.int32),
                pltpu.VMEM((tiles + 2 * halves + 1, width, 128), f32),
                pltpu.VMEM((tiles, width, 128), f32),
                pltpu.SemaphoreType.DMA,
            ],
            APPLY_LIMIT,
            "apply",
        )(packs[e], sources, fields)
        parts[e] = trade(result, e) if e else result
    out = pl.pallas_call(
        functools.partial(unpack_kernel, geometry),
        out_shape=jax.ShapeDtypeStruct((local_u * layers * ny, nz), f32),
        in_specs=vmem(chips),
        out_specs=pl.BlockSpec(memory_space=pl.ANY),
        scratch_shapes=[
            pltpu.VMEM((chips, tiles, local_u, 128), f32),
            pltpu.VMEM((local_u * layers * ny, nz), f32),
            pltpu.SemaphoreType.DMA((PIECES,)),
        ],
        compiler_params=pltpu.CompilerParams(vmem_limit_bytes=UNPACK_LIMIT * 1024 * 1024),
        name="unpack",
    )(*parts)
    return out.reshape(solution_modes.shape)


def solution(mesh):
    placed = (
        P("modes", "tiles", None, None),
        P("modes", "tiles", None, None),
        P("modes", None, None, None),
        P("modes", None),
        P("modes", None),
    )
    return jax.shard_map(
        on_device,
        mesh=mesh,
        in_specs=placed,
        out_specs=P("modes", "tiles", None, None),
        check_vma=False,
    )
```

```python
import functools

import jax
import jax.numpy as jnp
from jax import lax
from jax.experimental import pallas as pl
from jax.experimental.pallas import tpu as pltpu
from jax.sharding import PartitionSpec as P

PACK_LIMIT = 60
PREPARE_LIMIT = 24
UNPACK_LIMIT = 16
APPLY_LIMIT = 24
CHUNK = 4
PIECES = 4


def lane_index(rows):
    return lax.broadcasted_iota(jnp.int32, (rows, 128), 1)


def swap_lanes(tiles, depth, lanes):
    tiles = list(tiles)
    size = len(tiles)
    step = 1
    while step < size:
        width = step * depth
        upper = (lanes & width) != 0
        for low in range(size):
            if low & step:
                continue
            high = low | step
            first, second = tiles[low], tiles[high]
            tiles[low] = jnp.where(upper, pltpu.roll(second, width, 1), first)
            tiles[high] = jnp.where(upper, second, pltpu.roll(first, 128 - width, 1))
        step *= 2
    return tiles


def turn(value, shift):
    shift = shift % 128
    return value if shift == 0 else pltpu.roll(value, shift, 1)


def pack_kernel(geometry, u_hbm, a_hbm, *rest):
    layers, halves, ny, depth, chips = geometry
    sends, (stage, u_ref, a_ref, sems) = rest[:chips], rest[chips:]
    me = lax.axis_index("modes") // 2
    rows_u = u_ref.shape[0] // PIECES
    pairs = [(a_hbm, a_ref)]
    pairs += [(u_hbm.at[pl.ds(i * rows_u, rows_u)], u_ref.at[pl.ds(i * rows_u, rows_u)]) for i in range(PIECES)]
    copies = [pltpu.make_async_copy(one, two, sems.at[i]) for i, (one, two) in enumerate(pairs)]
    for copy in copies:
        copy.start()
    lanes = lane_index(8)
    place = lanes % depth
    cells = layers * ny

    def regroup(ref, first, count, target):
        def group(g, carry):
            to = pl.multiple_of(target + g * 8, 8)
            by_layer = []
            for x in range(layers):
                tiles = [ref[pl.ds((first + g * 8) * cells + x * ny + y, 8, stride=cells), :] for y in range(ny)]
                tiles = swap_lanes(tiles, depth, lanes)
                by_layer.append(tiles)
                for d in range(ny):
                    stage[d // halves, x * halves + d % halves, pl.ds(to, 8), :] = tiles[d]
            for chip in range(chips):
                rim = jnp.zeros((8, 128), jnp.float32)
                left, right = chip * halves - 1, (chip + 1) * halves
                for x in range(layers):
                    if left >= 0:
                        rim = jnp.where(place == x, turn(by_layer[x][left], x + 1 - depth), rim)
                    if right < ny:
                        at = depth // 2 + x
                        rim = jnp.where(place == at, turn(by_layer[x][right], at), rim)
                stage[chip, layers * halves, pl.ds(to, 8), :] = rim
            return carry

        lax.fori_loop(0, count // 8, group, 0, unroll=True)
        for e in range(chips):
            rows = pl.ds(target, count)
            copy = pltpu.make_async_copy(
                stage.at[e ^ me, :, rows], sends[e].at[:, rows], sems.at[len(copies) + len(sent)]
            )
            copy.start()
            sent.append(copy)

    sent = []
    local_a, local_u = a_ref.shape[0] // cells, u_ref.shape[0] // cells
    copies[0].wait()
    regroup(a_ref, 0, local_a, local_u)
    for i in range(PIECES):
        copies[1 + i].wait()
        regroup(u_ref, i * (local_u // PIECES), local_u // PIECES, i * (local_u // PIECES))
    for copy in sent:
        copy.wait()


def pack_coupling(coupling_ref, source_ref, expansion_ref, pack):
    blocks, slots, width, _ = coupling_ref.shape
    per = 128 // width
    groups = slots // per
    half = blocks * groups // 2
    for n in range(blocks * groups):
        rows = slice(n % half * width, (n % half + 1) * width)
        block, g = n // groups, n % groups
        pack[n // half, rows, :] = jnp.concatenate(
            [coupling_ref[block, g * per + q] for q in range(per)], axis=1
        )
    last = half * width
    pack[:, last : last + 8, :] = jnp.zeros((2, 8, 128), jnp.float32)
    pack[0, last : last + blocks, 0:slots] = source_ref[...].astype(jnp.float32)
    pack[0, last + blocks : last + 2 * blocks, 0:slots] = expansion_ref[...].astype(jnp.float32)


def laplacian(tile, low, high, rim, geometry, rows):
    layers, halves, ny, depth, _ = geometry
    lanes = lane_index(rows)
    place = lanes % depth
    first_row, last_row = lanes < depth, lanes >= 128 - depth
    result = []
    for x in range(layers):
        result.append([])
        for h in range(halves):
            c = tile[x][h]
            before = tile[x - 1][h] if x else low[h]
            after = tile[x + 1][h] if x + 1 < layers else high[h]
            up = jnp.where(first_row, 0.0, turn(c, depth))
            down = jnp.where(last_row, 0.0, turn(c, -depth))
            edge = turn(tile[x][h - 1], 1 - depth) if h else turn(rim, -x)
            left = jnp.where(place == 0, edge, turn(c, 1))
            if h + 1 < halves:
                edge = turn(tile[x][h + 1], depth - 1)
            else:
                edge = turn(rim, depth - 1 - depth // 2 - x)
            right = jnp.where(place == depth - 1, edge, turn(c, -1))
            result[-1].append(((before + after) + (up + down)) + ((left + right) - 6.0 * c))
    return result


def halves_of(value):
    upper = value.astype(jnp.bfloat16)
    lower = (value - upper.astype(jnp.float32)).astype(jnp.bfloat16)
    return upper, lower


def columns(tile, tiles):
    base = (tile // CHUNK) * 2 * CHUNK * 128 + (tile % CHUNK) * 128
    return base, base + CHUNK * 128


def prepare_kernel(geometry, width, local_u, local_a, group, *rest):
    layers, halves, ny, depth, chips = geometry
    many = len(group)
    bodies, low_ref, high_ref, other = rest[:many], rest[many], rest[many + 1], rest[many + 2]
    sources, fields = rest[-2:]
    tiles = layers * halves
    rim_at = 2 * tiles * 128
    me = lax.axis_index("modes")

    for i, side in [(i, side) for i in range(many) for side in range(2)]:
        first = i * (tiles + 1)
        body = other.at[pl.ds(first, tiles + 1)] if side else bodies[i]
        first = many * (tiles + 1) + i * halves
        low = other.at[pl.ds(first, halves)] if side else low_ref.at[pl.ds(i * halves, halves)]
        first += many * halves
        high = other.at[pl.ds(first, halves)] if side else high_ref.at[pl.ds(i * halves, halves)]
        device = me ^ (2 * group[i]) ^ side

        def load(start, rows, body=body, low=low, high=high):
            part = pl.ds(start, rows)
            tile = [[body[x * halves + h, part, :] for h in range(halves)] for x in range(layers)]
            below = [low[h, part, :] for h in range(halves)]
            above = [high[h, part, :] for h in range(halves)]
            return tile, below, above, body[tiles, part, :]

        def prepare_u(g, carry, load=load, device=device):
            start = pl.multiple_of(g * 16, 16)
            tile, below, above, rim = load(start, 16)
            lap = laplacian(tile, below, above, rim, geometry, 16)
            block = device * (local_u // width) + (g * 16) // width
            row = pl.multiple_of((g * 16) % width, 16)

            def put(value, at):
                upper, lower = halves_of(value)
                where = pl.ds(at, 128)
                sources[block, pl.ds(row, 16), where] = upper
                sources[block, pl.ds(width + row, 16), where] = lower
                sources[block, pl.ds(2 * width + row, 16), where] = upper

            for t in range(tiles):
                x, h = t // halves, t % halves
                put(tile[x][h], columns(t, tiles)[0])
                put(lap[x][h], columns(t, tiles)[1])
            for h in range(halves):
                put(below[h], rim_at + h * 128)
                put(above[h], rim_at + (halves + h) * 128)
            put(rim, rim_at + 2 * halves * 128)
            return carry

        lax.fori_loop(0, local_u // 16, prepare_u, 0, unroll=4)
        tile, below, above, rim = load(local_u, local_a)
        lap = laplacian(tile, below, above, rim, geometry, local_a)
        rows = pl.ds(pl.multiple_of(device * local_a, local_a), local_a)
        for t in range(tiles):
            x, h = t // halves, t % halves
            fields[rows, pl.ds(columns(t, tiles)[0], 128)] = tile[x][h]
            fields[rows, pl.ds(columns(t, tiles)[1], 128)] = lap[x][h]
        for h in range(halves):
            fields[rows, pl.ds(rim_at + h * 128, 128)] = below[h]
            fields[rows, pl.ds(rim_at + (halves + h) * 128, 128)] = above[h]
        fields[rows, pl.ds(rim_at + 2 * halves * 128, 128)] = rim


def apply_kernel(geometry, blocks, slots, width, e, *rest):
    packs, (sources, fields, out_ref, mix, numbers, table, product, cross, sem) = rest[:-9], rest[-9:]
    layers, halves, ny, depth, chips = geometry
    tiles = layers * halves
    chunks = tiles // CHUNK
    span = CHUNK * 128
    rim_at = 2 * tiles * 128
    rims = (2 * halves + 1) * 128
    per = 128 // width
    rows = blocks * slots // per * width // 2
    if e:
        core = lax.axis_index("modes") % 2
        bits = chips.bit_length() - 1
        reverse = sum(((e >> i) & 1) << (bits - 1 - i) for i in range(bits))
        mine = packs[0][jnp.where(core == 0, e, reverse)]
        other = packs[1][jnp.where(core == 0, reverse, e)]
        first = jnp.where(core == 0, mine, other)
        second = jnp.where(core == 0, other, mine)
    else:
        first, second = packs[0][0], packs[0][1]
    numbers[...] = first[rows : rows + 8].astype(jnp.int32)
    copy = pltpu.make_async_copy(numbers, table, sem)
    copy.start()
    value = jnp.concatenate([first[:rows], second[:rows]], axis=0)
    upper, lower = halves_of(value)
    take = lax.broadcasted_iota(jnp.int32, (256, per * 128), 0)
    give = lax.broadcasted_iota(jnp.int32, (256, per * 128), 1)
    lane = give % 128
    wanted = (give // 128) * width + lane % width + jnp.where(lane >= 2 * width, 128, 0)
    chosen = jnp.where((take == wanted) & (lane < 3 * width), 1.0, 0.0).astype(jnp.bfloat16)
    mix[...] = jnp.dot(
        jnp.concatenate([upper, lower], axis=1), chosen, preferred_element_type=jnp.float32
    ).astype(jnp.bfloat16)
    copy.wait()

    def one_block(n, carry):
        def operands(s, first, count):
            j, k = table[n, s], table[blocks + n, s]
            group = pl.multiple_of((n * (slots // per) + s // per) * width, width)
            lanes = (s % per) * 128
            mixed = jnp.dot(
                mix[pl.ds(group, width), lanes : lanes + 3 * width],
                sources[j, :, first : first + count],
                preferred_element_type=jnp.float32,
            )
            return mixed, k

        for chunk in range(chunks):
            base = chunk * 2 * span
            total = jnp.zeros((width, span), jnp.float32)
            rest_total = jnp.zeros((width, span), jnp.float32)
            for s in range(slots):
                mixed, k = operands(s, base, 2 * span)
                field = fields[pl.ds(k, 1), base : base + span]
                bent = fields[pl.ds(k, 1), base + span : base + 2 * span]
                value, curve = mixed[:, :span], mixed[:, span:]
                total = total + field * value
                rest_total = rest_total + (bent * value - field * curve)
            for i in range(CHUNK):
                product[chunk * CHUNK + i] = total[:, i * 128 : (i + 1) * 128]
                cross[chunk * CHUNK + i] = rest_total[:, i * 128 : (i + 1) * 128]

        total = jnp.zeros((width, rims), jnp.float32)
        for s in range(slots):
            mixed, k = operands(s, rim_at, rims)
            total = total + fields[pl.ds(k, 1), rim_at : rim_at + rims] * mixed
        for i in range(2 * halves + 1):
            product[tiles + i] = total[:, i * 128 : (i + 1) * 128]

        for r in range(0, width, 8):
            part = slice(r, r + 8)
            tile = [[product[x * halves + h, part, :] for h in range(halves)] for x in range(layers)]
            low = [product[tiles + h, part, :] for h in range(halves)]
            high = [product[tiles + halves + h, part, :] for h in range(halves)]
            rim = product[tiles + 2 * halves, part, :]
            lap = laplacian(tile, low, high, rim, geometry, 8)
            for t in range(tiles):
                row = pl.multiple_of(n * width + r, 8)
                out_ref[t, pl.ds(row, 8), :] = 0.5 * (
                    cross[t, part, :] - lap[t // halves][t % halves]
                )
        return carry

    lax.fori_loop(0, blocks, one_block, 0, unroll=True)


def unpack_kernel(geometry, *rest):
    layers, halves, ny, depth, chips = geometry
    parts, out_hbm = rest[:chips], rest[chips]
    stage, out_ref, sems = rest[chips + 1 :]
    me = lax.axis_index("modes") // 2
    for e in range(chips):
        stage[e ^ me] = parts[e][...]
    lanes = lane_index(8)
    cells = layers * ny
    modes = out_ref.shape[0] // cells
    size = modes // PIECES

    def group(g, carry):
        source = pl.multiple_of(g * 8, 8)
        for x in range(layers):
            tiles = [stage[d // halves, x * halves + d % halves, pl.ds(source, 8), :] for d in range(ny)]
            tiles = swap_lanes(tiles, depth, lanes)
            for y in range(ny):
                out_ref[pl.ds(g * 8 * cells + x * ny + y, 8, stride=cells), :] = tiles[y]
        return carry

    copies = []
    for i in range(PIECES):
        lax.fori_loop(i * size // 8, (i + 1) * size // 8, group, 0)
        rows = pl.ds(i * size * cells, size * cells)
        copies.append(pltpu.make_async_copy(out_ref.at[rows], out_hbm.at[rows], sems.at[i]))
        copies[-1].start()
    for copy in copies:
        copy.wait()


def vmem(count):
    return [pl.BlockSpec(memory_space=pltpu.VMEM)] * count


def on_device(solution_modes, coefficient_modes, coupling, source_block, expansion_index):
    local_u, layers, ny, nz = solution_modes.shape
    local_a = coefficient_modes.shape[0]
    blocks, slots, width = coupling.shape[:3]
    count = lax.axis_size("modes")
    chips = count // 2
    depth = 128 // ny
    halves = (nz // depth) // chips
    geometry = (layers, halves, ny, depth, chips)
    tiles = layers * halves
    modes = local_u + local_a
    f32 = jnp.float32

    def call(kernel, shapes, inputs, scratch, limit, name, **more):
        return pl.pallas_call(
            kernel,
            out_shape=shapes,
            in_specs=vmem(inputs),
            out_specs=jax.tree.map(lambda _: pl.BlockSpec(memory_space=pltpu.VMEM), shapes),
            scratch_shapes=scratch,
            compiler_params=pltpu.CompilerParams(vmem_limit_bytes=limit * 1024 * 1024),
            name=name,
            **more,
        )

    rows = blocks * slots * width // (128 // width)
    sends = pl.pallas_call(
        functools.partial(pack_kernel, geometry),
        out_shape=[jax.ShapeDtypeStruct((tiles + 1, modes, 128), f32)] * chips,
        in_specs=[pl.BlockSpec(memory_space=pltpu.HBM)] * 2,
        out_specs=[pl.BlockSpec(memory_space=pltpu.HBM)] * chips,
        scratch_shapes=[
            pltpu.VMEM((chips, tiles + 1, modes, 128), f32),
            pltpu.VMEM((local_u * layers * ny, nz), f32),
            pltpu.VMEM((local_a * layers * ny, nz), f32),
            pltpu.SemaphoreType.DMA((PIECES + 1 + chips * (PIECES + 1),)),
        ],
        compiler_params=pltpu.CompilerParams(vmem_limit_bytes=PACK_LIMIT * 1024 * 1024),
        name="pack",
    )(
        solution_modes.reshape(-1, nz),
        coefficient_modes.reshape(-1, nz),
    )
    pack = call(
        pack_coupling,
        jax.ShapeDtypeStruct((2, rows // 2 + 8, 128), f32),
        3,
        [],
        UNPACK_LIMIT,
        "pack_coupling",
    )(coupling, source_block, expansion_index)

    def trade(value, e):
        return lax.ppermute(value, "modes", [(i, i ^ (2 * e)) for i in range(count)])

    def sibling(value):
        return lax.ppermute(value, "modes", [(i, i ^ 1) for i in range(count)])

    bodies = [sends[0]] + [trade(sends[e], e) for e in range(1, chips)]
    n_tiles = lax.axis_size("tiles")
    up = [(i, i + 1) for i in range(n_tiles - 1)]
    down = [(i + 1, i) for i in range(n_tiles - 1)]
    gathered = []
    for group in ([0, chips - 1], list(range(1, chips - 1))):
        top = jnp.concatenate([bodies[e][tiles - halves : tiles] for e in group])
        bottom = jnp.concatenate([bodies[e][:halves] for e in group])
        low, high = lax.ppermute(top, "tiles", up), lax.ppermute(bottom, "tiles", down)
        mine = [bodies[e] for e in group] + [low, high]
        gathered.append((group, mine + [sibling(jnp.concatenate(mine))]))

    bits = chips.bit_length() - 1
    core = lax.axis_index("modes") % 2
    keep = lax.dynamic_index_in_dim(pack, core, 0)
    give = lax.dynamic_index_in_dim(pack, 1 - core, 0)
    held = jnp.concatenate([keep, sibling(give)])[None]
    for i in range(bits):
        if i == bits - 1:
            held = lax.optimization_barrier((held, gathered[0][1][-2]))[0]
        pairs = [(m, m ^ (2 << (i if m % 2 == 0 else bits - 1 - i))) for m in range(count)]
        held = jnp.concatenate([held, lax.ppermute(held, "modes", pairs)])
    packs = [held[:, 0], sibling(held[:, 1])]

    ncol = 2 * tiles * 128 + (2 * halves + 1) * 128
    n_blocks = count * (local_u // width)
    prepared = ()
    for group, inputs in gathered:
        prepared = call(
            functools.partial(prepare_kernel, geometry, width, local_u, local_a, group),
            (
                jax.ShapeDtypeStruct((n_blocks, 3 * width, ncol), jnp.bfloat16),
                jax.ShapeDtypeStruct((count * local_a, ncol), f32),
            ),
            len(inputs) + len(prepared),
            [],
            PREPARE_LIMIT,
            "prepare",
            input_output_aliases={len(inputs): 0, len(inputs) + 1: 1} if prepared else {},
        )(*inputs, *prepared)
    sources, fields = prepared

    parts = [None] * chips
    for e in list(range(chips - 1, -1, -1)):
        result = call(
            functools.partial(apply_kernel, geometry, blocks, slots, width, e),
            jax.ShapeDtypeStruct((tiles, local_u, 128), f32),
            4 if e else 3,
            [
                pltpu.VMEM((rows, 128 // width * 128), jnp.bfloat16),
                pltpu.VMEM((8, 128), jnp.int32),
                pltpu.SMEM((8, 128), jnp.int32),
                pltpu.VMEM((tiles + 2 * halves + 1, width, 128), f32),
                pltpu.VMEM((tiles, width, 128), f32),
                pltpu.SemaphoreType.DMA,
            ],
            APPLY_LIMIT,
            "apply",
        )(*(packs if e else [pack]), sources, fields)
        parts[e] = trade(result, e) if e else result
    out = pl.pallas_call(
        functools.partial(unpack_kernel, geometry),
        out_shape=jax.ShapeDtypeStruct((local_u * layers * ny, nz), f32),
        in_specs=vmem(chips),
        out_specs=pl.BlockSpec(memory_space=pl.ANY),
        scratch_shapes=[
            pltpu.VMEM((chips, tiles, local_u, 128), f32),
            pltpu.VMEM((local_u * layers * ny, nz), f32),
            pltpu.SemaphoreType.DMA((PIECES,)),
        ],
        compiler_params=pltpu.CompilerParams(vmem_limit_bytes=UNPACK_LIMIT * 1024 * 1024),
        name="unpack",
    )(*parts)
    return out.reshape(solution_modes.shape)


def solution(mesh):
    placed = (
        P("modes", "tiles", None, None),
        P("modes", "tiles", None, None),
        P("modes", None, None, None),
        P("modes", None),
        P("modes", None),
    )
    return jax.shard_map(
        on_device,
        mesh=mesh,
        in_specs=placed,
        out_specs=P("modes", "tiles", None, None),
        check_vma=False,
    )
```

```python
import functools

import jax
import jax.numpy as jnp
from jax import lax
from jax.experimental import pallas as pl
from jax.experimental.pallas import tpu as pltpu
from jax.sharding import PartitionSpec as P

PACK_LIMIT = 60
PREPARE_LIMIT = 24
UNPACK_LIMIT = 16
APPLY_LIMIT = 24
CHUNK = 4
PIECES = 4


def lane_index(rows):
    return lax.broadcasted_iota(jnp.int32, (rows, 128), 1)


def swap_lanes(tiles, depth, lanes):
    tiles = list(tiles)
    size = len(tiles)
    step = 1
    while step < size:
        width = step * depth
        upper = (lanes & width) != 0
        for low in range(size):
            if low & step:
                continue
            high = low | step
            first, second = tiles[low], tiles[high]
            tiles[low] = jnp.where(upper, pltpu.roll(second, width, 1), first)
            tiles[high] = jnp.where(upper, second, pltpu.roll(first, 128 - width, 1))
        step *= 2
    return tiles


def turn(value, shift):
    shift = shift % 128
    return value if shift == 0 else pltpu.roll(value, shift, 1)


def pack_kernel(geometry, u_hbm, a_hbm, *rest):
    layers, halves, ny, depth, chips = geometry
    sends, (stage, u_ref, a_ref, sems) = rest[:chips], rest[chips:]
    me = lax.axis_index("modes") // 2
    rows_u = u_ref.shape[0] // PIECES
    pairs = [(a_hbm, a_ref)]
    pairs += [(u_hbm.at[pl.ds(i * rows_u, rows_u)], u_ref.at[pl.ds(i * rows_u, rows_u)]) for i in range(PIECES)]
    copies = [pltpu.make_async_copy(one, two, sems.at[i]) for i, (one, two) in enumerate(pairs)]
    for copy in copies:
        copy.start()
    lanes = lane_index(8)
    place = lanes % depth
    cells = layers * ny

    def regroup(ref, first, count, target):
        def group(g, carry):
            to = pl.multiple_of(target + g * 8, 8)
            by_layer = []
            for x in range(layers):
                tiles = [ref[pl.ds((first + g * 8) * cells + x * ny + y, 8, stride=cells), :] for y in range(ny)]
                tiles = swap_lanes(tiles, depth, lanes)
                by_layer.append(tiles)
                for d in range(ny):
                    stage[d // halves, x * halves + d % halves, pl.ds(to, 8), :] = tiles[d]
            for chip in range(chips):
                rim = jnp.zeros((8, 128), jnp.float32)
                left, right = chip * halves - 1, (chip + 1) * halves
                for x in range(layers):
                    if left >= 0:
                        rim = jnp.where(place == x, turn(by_layer[x][left], x + 1 - depth), rim)
                    if right < ny:
                        at = depth // 2 + x
                        rim = jnp.where(place == at, turn(by_layer[x][right], at), rim)
                stage[chip, layers * halves, pl.ds(to, 8), :] = rim
            return carry

        lax.fori_loop(0, count // 8, group, 0, unroll=True)
        for e in range(chips):
            rows = pl.ds(target, count)
            copy = pltpu.make_async_copy(
                stage.at[e ^ me, :, rows], sends[e].at[:, rows], sems.at[len(copies) + len(sent)]
            )
            copy.start()
            sent.append(copy)

    sent = []
    local_a, local_u = a_ref.shape[0] // cells, u_ref.shape[0] // cells
    copies[0].wait()
    regroup(a_ref, 0, local_a, local_u)
    for i in range(PIECES):
        copies[1 + i].wait()
        regroup(u_ref, i * (local_u // PIECES), local_u // PIECES, i * (local_u // PIECES))
    for copy in sent:
        copy.wait()


def pack_coupling(coupling_ref, source_ref, expansion_ref, pack, select):
    blocks, slots, width, _ = coupling_ref.shape
    per = 128 // width
    groups = slots // per
    half = blocks * groups // 2
    for n in range(blocks * groups):
        rows = slice(n % half * width, (n % half + 1) * width)
        block, g = n // groups, n % groups
        pack[n // half, rows, :] = jnp.concatenate(
            [coupling_ref[block, g * per + q] for q in range(per)], axis=1
        )
    last = half * width
    pack[:, last : last + 8, :] = jnp.zeros((2, 8, 128), jnp.float32)
    pack[0, last : last + blocks, 0:slots] = source_ref[...].astype(jnp.float32)
    pack[0, last + blocks : last + 2 * blocks, 0:slots] = expansion_ref[...].astype(jnp.float32)
    take = lax.broadcasted_iota(jnp.int32, (256, per * 128), 0)
    give = lax.broadcasted_iota(jnp.int32, (256, per * 128), 1)
    lane = give % 128
    wanted = (give // 128) * width + lane % width + jnp.where(lane >= 2 * width, 128, 0)
    select[...] = jnp.where((take == wanted) & (lane < 3 * width), 1.0, 0.0).astype(jnp.bfloat16)


def laplacian(tile, low, high, rim, geometry, rows):
    layers, halves, ny, depth, _ = geometry
    lanes = lane_index(rows)
    place = lanes % depth
    first_row, last_row = lanes < depth, lanes >= 128 - depth
    result = []
    for x in range(layers):
        result.append([])
        for h in range(halves):
            c = tile[x][h]
            before = tile[x - 1][h] if x else low[h]
            after = tile[x + 1][h] if x + 1 < layers else high[h]
            up = jnp.where(first_row, 0.0, turn(c, depth))
            down = jnp.where(last_row, 0.0, turn(c, -depth))
            edge = turn(tile[x][h - 1], 1 - depth) if h else turn(rim, -x)
            left = jnp.where(place == 0, edge, turn(c, 1))
            if h + 1 < halves:
                edge = turn(tile[x][h + 1], depth - 1)
            else:
                edge = turn(rim, depth - 1 - depth // 2 - x)
            right = jnp.where(place == depth - 1, edge, turn(c, -1))
            result[-1].append(((before + after) + (up + down)) + ((left + right) - 6.0 * c))
    return result


def halves_of(value):
    upper = value.astype(jnp.bfloat16)
    lower = (value - upper.astype(jnp.float32)).astype(jnp.bfloat16)
    return upper, lower


def columns(tile, tiles):
    base = (tile // CHUNK) * 2 * CHUNK * 128 + (tile % CHUNK) * 128
    return base, base + CHUNK * 128


def prepare_kernel(geometry, width, local_u, local_a, group, *rest):
    layers, halves, ny, depth, chips = geometry
    many = len(group)
    bodies, low_ref, high_ref, other = rest[:many], rest[many], rest[many + 1], rest[many + 2]
    sources, fields = rest[-2:]
    tiles = layers * halves
    rim_at = 2 * tiles * 128
    me = lax.axis_index("modes")

    for i, side in [(i, side) for i in range(many) for side in range(2)]:
        first = i * (tiles + 1)
        body = other.at[pl.ds(first, tiles + 1)] if side else bodies[i]
        first = many * (tiles + 1) + i * halves
        low = other.at[pl.ds(first, halves)] if side else low_ref.at[pl.ds(i * halves, halves)]
        first += many * halves
        high = other.at[pl.ds(first, halves)] if side else high_ref.at[pl.ds(i * halves, halves)]
        device = me ^ (2 * group[i]) ^ side

        def load(start, rows, body=body, low=low, high=high):
            part = pl.ds(start, rows)
            tile = [[body[x * halves + h, part, :] for h in range(halves)] for x in range(layers)]
            below = [low[h, part, :] for h in range(halves)]
            above = [high[h, part, :] for h in range(halves)]
            return tile, below, above, body[tiles, part, :]

        def prepare_u(g, carry, load=load, device=device):
            start = pl.multiple_of(g * 16, 16)
            tile, below, above, rim = load(start, 16)
            lap = laplacian(tile, below, above, rim, geometry, 16)
            block = device * (local_u // width) + (g * 16) // width
            row = pl.multiple_of((g * 16) % width, 16)

            def put(value, at):
                upper, lower = halves_of(value)
                where = pl.ds(at, 128)
                sources[block, pl.ds(row, 16), where] = upper
                sources[block, pl.ds(width + row, 16), where] = lower
                sources[block, pl.ds(2 * width + row, 16), where] = upper

            for t in range(tiles):
                x, h = t // halves, t % halves
                put(tile[x][h], columns(t, tiles)[0])
                put(lap[x][h], columns(t, tiles)[1])
            for h in range(halves):
                put(below[h], rim_at + h * 128)
                put(above[h], rim_at + (halves + h) * 128)
            put(rim, rim_at + 2 * halves * 128)
            return carry

        lax.fori_loop(0, local_u // 16, prepare_u, 0, unroll=4)
        tile, below, above, rim = load(local_u, local_a)
        lap = laplacian(tile, below, above, rim, geometry, local_a)
        rows = pl.ds(pl.multiple_of(device * local_a, local_a), local_a)
        for t in range(tiles):
            x, h = t // halves, t % halves
            fields[rows, pl.ds(columns(t, tiles)[0], 128)] = tile[x][h]
            fields[rows, pl.ds(columns(t, tiles)[1], 128)] = lap[x][h]
        for h in range(halves):
            fields[rows, pl.ds(rim_at + h * 128, 128)] = below[h]
            fields[rows, pl.ds(rim_at + (halves + h) * 128, 128)] = above[h]
        fields[rows, pl.ds(rim_at + 2 * halves * 128, 128)] = rim


def apply_kernel(geometry, blocks, slots, width, e, *rest):
    packs, (chosen, sources, fields, out_ref, mix, numbers, table, product, cross, sem) = rest[:-10], rest[-10:]
    layers, halves, ny, depth, chips = geometry
    tiles = layers * halves
    chunks = tiles // CHUNK
    span = CHUNK * 128
    rim_at = 2 * tiles * 128
    rims = (2 * halves + 1) * 128
    per = 128 // width
    rows = blocks * slots // per * width // 2
    if e:
        core = lax.axis_index("modes") % 2
        bits = chips.bit_length() - 1
        reverse = sum(((e >> i) & 1) << (bits - 1 - i) for i in range(bits))
        mine = packs[0][jnp.where(core == 0, e, reverse)]
        other = packs[1][jnp.where(core == 0, reverse, e)]
        first = jnp.where(core == 0, mine, other)
        second = jnp.where(core == 0, other, mine)
    else:
        first, second = packs[0][0], packs[0][1]
    numbers[...] = first[rows : rows + 8].astype(jnp.int32)
    copy = pltpu.make_async_copy(numbers, table, sem)
    copy.start()
    value = jnp.concatenate([first[:rows], second[:rows]], axis=0)
    upper, lower = halves_of(value)
    mix[...] = jnp.dot(
        jnp.concatenate([upper, lower], axis=1), chosen[...], preferred_element_type=jnp.float32
    ).astype(jnp.bfloat16)
    copy.wait()

    def one_block(n, carry):
        def operands(s, first, count):
            j, k = table[n, s], table[blocks + n, s]
            group = pl.multiple_of((n * (slots // per) + s // per) * width, width)
            lanes = (s % per) * 128
            mixed = jnp.dot(
                mix[pl.ds(group, width), lanes : lanes + 3 * width],
                sources[j, :, first : first + count],
                preferred_element_type=jnp.float32,
            )
            return mixed, k

        for chunk in range(chunks):
            base = chunk * 2 * span
            total = jnp.zeros((width, span), jnp.float32)
            rest_total = jnp.zeros((width, span), jnp.float32)
            for s in range(slots):
                mixed, k = operands(s, base, 2 * span)
                field = fields[pl.ds(k, 1), base : base + span]
                bent = fields[pl.ds(k, 1), base + span : base + 2 * span]
                value, curve = mixed[:, :span], mixed[:, span:]
                total = total + field * value
                rest_total = rest_total + (bent * value - field * curve)
            for i in range(CHUNK):
                product[chunk * CHUNK + i] = total[:, i * 128 : (i + 1) * 128]
                cross[chunk * CHUNK + i] = rest_total[:, i * 128 : (i + 1) * 128]

        total = jnp.zeros((width, rims), jnp.float32)
        for s in range(slots):
            mixed, k = operands(s, rim_at, rims)
            total = total + fields[pl.ds(k, 1), rim_at : rim_at + rims] * mixed
        for i in range(2 * halves + 1):
            product[tiles + i] = total[:, i * 128 : (i + 1) * 128]

        for r in range(0, width, 8):
            part = slice(r, r + 8)
            tile = [[product[x * halves + h, part, :] for h in range(halves)] for x in range(layers)]
            low = [product[tiles + h, part, :] for h in range(halves)]
            high = [product[tiles + halves + h, part, :] for h in range(halves)]
            rim = product[tiles + 2 * halves, part, :]
            lap = laplacian(tile, low, high, rim, geometry, 8)
            for t in range(tiles):
                row = pl.multiple_of(n * width + r, 8)
                out_ref[t, pl.ds(row, 8), :] = 0.5 * (
                    cross[t, part, :] - lap[t // halves][t % halves]
                )
        return carry

    lax.fori_loop(0, blocks, one_block, 0, unroll=True)


def unpack_kernel(geometry, *rest):
    layers, halves, ny, depth, chips = geometry
    parts, out_hbm = rest[:chips], rest[chips]
    stage, out_ref, sems = rest[chips + 1 :]
    me = lax.axis_index("modes") // 2
    for e in range(chips):
        stage[e ^ me] = parts[e][...]
    lanes = lane_index(8)
    cells = layers * ny
    modes = out_ref.shape[0] // cells
    size = modes // PIECES

    def group(g, carry):
        source = pl.multiple_of(g * 8, 8)
        for x in range(layers):
            tiles = [stage[d // halves, x * halves + d % halves, pl.ds(source, 8), :] for d in range(ny)]
            tiles = swap_lanes(tiles, depth, lanes)
            for y in range(ny):
                out_ref[pl.ds(g * 8 * cells + x * ny + y, 8, stride=cells), :] = tiles[y]
        return carry

    copies = []
    for i in range(PIECES):
        lax.fori_loop(i * size // 8, (i + 1) * size // 8, group, 0)
        rows = pl.ds(i * size * cells, size * cells)
        copies.append(pltpu.make_async_copy(out_ref.at[rows], out_hbm.at[rows], sems.at[i]))
        copies[-1].start()
    for copy in copies:
        copy.wait()


def vmem(count):
    return [pl.BlockSpec(memory_space=pltpu.VMEM)] * count


def on_device(solution_modes, coefficient_modes, coupling, source_block, expansion_index):
    local_u, layers, ny, nz = solution_modes.shape
    local_a = coefficient_modes.shape[0]
    blocks, slots, width = coupling.shape[:3]
    count = lax.axis_size("modes")
    chips = count // 2
    depth = 128 // ny
    halves = (nz // depth) // chips
    geometry = (layers, halves, ny, depth, chips)
    tiles = layers * halves
    modes = local_u + local_a
    f32 = jnp.float32

    def call(kernel, shapes, inputs, scratch, limit, name, **more):
        return pl.pallas_call(
            kernel,
            out_shape=shapes,
            in_specs=vmem(inputs),
            out_specs=jax.tree.map(lambda _: pl.BlockSpec(memory_space=pltpu.VMEM), shapes),
            scratch_shapes=scratch,
            compiler_params=pltpu.CompilerParams(vmem_limit_bytes=limit * 1024 * 1024),
            name=name,
            **more,
        )

    rows = blocks * slots * width // (128 // width)
    sends = pl.pallas_call(
        functools.partial(pack_kernel, geometry),
        out_shape=[jax.ShapeDtypeStruct((tiles + 1, modes, 128), f32)] * chips,
        in_specs=[pl.BlockSpec(memory_space=pltpu.HBM)] * 2,
        out_specs=[pl.BlockSpec(memory_space=pltpu.HBM)] * chips,
        scratch_shapes=[
            pltpu.VMEM((chips, tiles + 1, modes, 128), f32),
            pltpu.VMEM((local_u * layers * ny, nz), f32),
            pltpu.VMEM((local_a * layers * ny, nz), f32),
            pltpu.SemaphoreType.DMA((PIECES + 1 + chips * (PIECES + 1),)),
        ],
        compiler_params=pltpu.CompilerParams(vmem_limit_bytes=PACK_LIMIT * 1024 * 1024),
        name="pack",
    )(
        solution_modes.reshape(-1, nz),
        coefficient_modes.reshape(-1, nz),
    )
    pack, select = call(
        pack_coupling,
        [
            jax.ShapeDtypeStruct((2, rows // 2 + 8, 128), f32),
            jax.ShapeDtypeStruct((256, 128 // width * 128), jnp.bfloat16),
        ],
        3,
        [],
        UNPACK_LIMIT,
        "pack_coupling",
    )(coupling, source_block, expansion_index)

    def trade(value, e):
        return lax.ppermute(value, "modes", [(i, i ^ (2 * e)) for i in range(count)])

    def sibling(value):
        return lax.ppermute(value, "modes", [(i, i ^ 1) for i in range(count)])

    bodies = [sends[0]] + [trade(sends[e], e) for e in range(1, chips)]
    n_tiles = lax.axis_size("tiles")
    up = [(i, i + 1) for i in range(n_tiles - 1)]
    down = [(i + 1, i) for i in range(n_tiles - 1)]
    gathered = []
    for group in ([0, chips - 1], list(range(1, chips - 1))):
        top = jnp.concatenate([bodies[e][tiles - halves : tiles] for e in group])
        bottom = jnp.concatenate([bodies[e][:halves] for e in group])
        low, high = lax.ppermute(top, "tiles", up), lax.ppermute(bottom, "tiles", down)
        mine = [bodies[e] for e in group] + [low, high]
        gathered.append((group, mine + [sibling(jnp.concatenate(mine))]))

    bits = chips.bit_length() - 1
    core = lax.axis_index("modes") % 2
    keep = lax.dynamic_index_in_dim(pack, core, 0)
    give = lax.dynamic_index_in_dim(pack, 1 - core, 0)
    held = jnp.concatenate([keep, sibling(give)])[None]
    for i in range(bits):
        if i == bits - 1:
            held = lax.optimization_barrier((held, gathered[0][1][-2]))[0]
        pairs = [(m, m ^ (2 << (i if m % 2 == 0 else bits - 1 - i))) for m in range(count)]
        held = jnp.concatenate([held, lax.ppermute(held, "modes", pairs)])
    packs = [held[:, 0], sibling(held[:, 1])]

    ncol = 2 * tiles * 128 + (2 * halves + 1) * 128
    n_blocks = count * (local_u // width)
    prepared = ()
    for group, inputs in gathered:
        prepared = call(
            functools.partial(prepare_kernel, geometry, width, local_u, local_a, group),
            (
                jax.ShapeDtypeStruct((n_blocks, 3 * width, ncol), jnp.bfloat16),
                jax.ShapeDtypeStruct((count * local_a, ncol), f32),
            ),
            len(inputs) + len(prepared),
            [],
            PREPARE_LIMIT,
            "prepare",
            input_output_aliases={len(inputs): 0, len(inputs) + 1: 1} if prepared else {},
        )(*inputs, *prepared)
    sources, fields = prepared

    parts = [None] * chips
    for e in list(range(chips - 1, -1, -1)):
        result = call(
            functools.partial(apply_kernel, geometry, blocks, slots, width, e),
            jax.ShapeDtypeStruct((tiles, local_u, 128), f32),
            5 if e else 4,
            [
                pltpu.VMEM((rows, 128 // width * 128), jnp.bfloat16),
                pltpu.VMEM((8, 128), jnp.int32),
                pltpu.SMEM((8, 128), jnp.int32),
                pltpu.VMEM((tiles + 2 * halves + 1, width, 128), f32),
                pltpu.VMEM((tiles, width, 128), f32),
                pltpu.SemaphoreType.DMA,
            ],
            APPLY_LIMIT,
            "apply",
        )(*(packs if e else [pack]), select, sources, fields)
        parts[e] = trade(result, e) if e else result
    out = pl.pallas_call(
        functools.partial(unpack_kernel, geometry),
        out_shape=jax.ShapeDtypeStruct((local_u * layers * ny, nz), f32),
        in_specs=vmem(chips),
        out_specs=pl.BlockSpec(memory_space=pl.ANY),
        scratch_shapes=[
            pltpu.VMEM((chips, tiles, local_u, 128), f32),
            pltpu.VMEM((local_u * layers * ny, nz), f32),
            pltpu.SemaphoreType.DMA((PIECES,)),
        ],
        compiler_params=pltpu.CompilerParams(vmem_limit_bytes=UNPACK_LIMIT * 1024 * 1024),
        name="unpack",
    )(*parts)
    return out.reshape(solution_modes.shape)


def solution(mesh):
    placed = (
        P("modes", "tiles", None, None),
        P("modes", "tiles", None, None),
        P("modes", None, None, None),
        P("modes", None),
        P("modes", None),
    )
    return jax.shard_map(
        on_device,
        mesh=mesh,
        in_specs=placed,
        out_specs=P("modes", "tiles", None, None),
        check_vma=False,
    )
```
